32 devices in a mesh: wide: 8 (over z, y), narrow: 4 (over x, core).
Axes of the slice: x: 2, y: 2, z: 4, core: 2. Of those that a mesh axis runs over, the one named last changes fastest.
Arguments:
- items: bfloat16 [16384, 256], P(('wide', 'narrow')), may hold values from -6 to 6
- tile1_values: bfloat16 [384, 128, 128], P(('wide', 'narrow')), may hold values from -0.3125 to 0.3125
- tile1_source: int32 [384], P(('wide', 'narrow')), may hold values from 0 to 3
- tile1_owner: int32 [384, 1], P(('wide', 'narrow')), may hold values from 0 to 7; in each aligned block of 12 rows (0 to 11, 12 to 23, ...) at most 2 rows name the same one
- tile1_slot: int32 [384], P(('wide', 'narrow')), may hold values from 0 to 3
- tile2_values: bfloat16 [384, 128, 128], P(('wide', 'narrow')), may hold values from -0.3125 to 0.3125
- tile2_source: int32 [384], P(('wide', 'narrow')), may hold values from 0 to 3
- tile2_owner: int32 [384, 1], P(('wide', 'narrow')), may hold values from 0 to 7; in each aligned block of 12 rows (0 to 11, 12 to 23, ...) at most 2 rows name the same one
- tile2_slot: int32 [384], P(('wide', 'narrow')), may hold values from 0 to 15
- weight: bfloat16 [256, 256], replicated, may hold values from -0.375 to 0.375
- bundle_degree: int32 [16384], P(('wide', 'narrow')), may hold values from 1 to 4
- user_degree: int32 [16384], P('wide'), may hold values from 1 to 4
- cotangent: bfloat16 [16384, 256], P('wide'), may hold values from -6 to 6
Outputs:
- user_out: bfloat16 [16384, 256], P('wide')
- grad_weight: float32 [256, 256], replicated
- grad_bundle: bfloat16 [16384, 256], P(('wide', 'narrow'))
The draws below stay inside these ranges and needn't reach their ends.
Inputs may be any that keep to these rules, and one draw needn't show every extreme that they name: `tile1_owner`: among the 12 tiles of one device, at most 2 name the same owner, a bound that some block reaches. `tile2_owner`: among the 12 tiles of one device, at most 2 name the same owner, a bound that some block reaches.
All inputs are finite; a program needn't handle non-finite values.
Results may differ from the reference program's by a relative error of at most 0.0073.
Values may be sent and summed in bfloat16 or wider, within the bound.
A program may use at most 128 MiB of HBM per device.

```python
import math
import jax
import jax.numpy as jnp
import numpy as np
from jax import lax

F = 256
TILE = 128
CAP = 2
IB_DEV = 4
BB_DEV = 4
UGRP = 16
TILES1 = 12
TILES_ALL = 384
ITEMS = 16384
BUNDLES = 16384
USERS = 16384
N_WIDE = 8
N_NARROW = 4
DEVICES = 32


def place_ends(result, rng, low, largest):
    index_at = [jax.random.randint(jax.random.fold_in(rng, axis), (), 0, length) for axis, length in enumerate(result.shape)]
    longest = result.shape.index(max(result.shape))
    next_to = index_at[:longest] + [(index_at[longest] + 1) % result.shape[longest]] + index_at[longest + 1:]
    return result.at[tuple(index_at)].set(low).at[tuple(next_to)].set(largest)


def block_levels(own_key, extent, cuts, least, largest):
    loudness = 1.0
    for axis_at, shards_of in cuts:
        draws = jax.random.uniform(jax.random.fold_in(jax.random.fold_in(own_key, 6), axis_at), (shards_of,), jnp.float32, least / len(cuts), largest / len(cuts))
        loudness = loudness * jnp.repeat(jnp.exp(draws), extent[axis_at] // shards_of).reshape((-1,) + (1,) * (len(extent) - 1 - axis_at))
    return loudness


def assign_block(rng, own, number, rows, amount, top, most, slope):
    order = jax.random.permutation(rng, amount)
    heavy_load, common = shares(amount, rows * top, most, slope, True), shares(amount, rows * top, most, slope, False)
    places = jnp.arange(amount)

    def named(sizes, rotation):
        used = int((sizes > 0).sum())
        fixed = max(1, used // 4)
        moved = fixed + (places - fixed + rotation * (used - fixed)) % max(1, amount - fixed)
        return jnp.zeros((amount,), jnp.int32).at[order[jnp.where(places < fixed, places, moved)]].set(jnp.asarray(sizes, jnp.int32))

    sizes = jnp.where(number % 4 == 0, named(heavy_load, number // 4), named(common, number - number // 4 - 1))
    mixed = jax.random.permutation(jax.random.fold_in(own, 3), amount)
    source_of, taker = mixed[0:amount // 2 * 2:2], mixed[1:amount // 2 * 2:2]
    slack = jnp.minimum(sizes[source_of] - 1, most - sizes[taker]) // 2
    slack = jnp.where((source_of == order[0]) | (taker == order[0]) | (sizes[taker] == 0), 0, jnp.maximum(slack, 0))
    moved = jax.random.randint(jax.random.fold_in(own, 4), (amount // 2,), 0, 1 << 20) % (slack + 1)
    sizes = sizes.at[source_of].add(-moved).at[taker].add(moved)
    labels = jnp.searchsorted(jnp.cumsum(sizes), jnp.arange(rows * top), side="right").astype(jnp.int32)
    listing = labels.reshape(top, rows).T
    listing = listing[jax.random.permutation(jax.random.fold_in(own, 1), rows)]
    rotation = jax.random.randint(jax.random.fold_in(own, 2), (rows, 1), 0, top)
    return jnp.take_along_axis(listing, (jnp.arange(top)[None, :] + rotation) % top, axis=1)


def shares(amount, total, most, skew, full):
    weights = [(1 << 20) // math.isqrt(standing ** skew) + 1 for standing in range(1, amount + 1)]
    largest = most if full else min(most, max(-(-total // amount), total * weights[0] // sum(weights)))
    least = 1 if total - largest >= amount - 1 else 0
    given, rest = [largest] + [least] * (amount - 1), total - largest - least * (amount - 1)
    while rest > 0:
        free = [i for i in range(1, amount) if given[i] < largest] or [i for i in range(1, amount) if given[i] < most]
        pool, remaining = sum([weights[i] for i in free]), rest
        for i in free:
            addition = min(most - given[i], max(1, remaining * weights[i] // pool), rest)
            given[i] = given[i] + addition
            rest = rest - addition
    return np.array(given)


def normal_values(key, dims, scale, reach, split=(), kind=jnp.bfloat16):
    entries = jax.random.normal(key, dims, jnp.float32) * scale
    if len(split) > 0:
        entries = block_levels(key, dims, split, -0.22, 0.18) * entries
    return jnp.clip(entries, min=-reach, max=reach).astype(kind)


def setup_inputs(seed: int = 0) -> dict:
    splits = jax.random.split(jax.random.key(seed), 14)
    items = normal_values(splits[0], (ITEMS, F), 1.0, 6.0, ((0, 32),))
    tile1_values = normal_values(splits[1], (TILES_ALL, TILE, TILE), (TILE * TILES1 // BB_DEV) ** -0.5, 0.3125, ((0, 32),))
    tile1_source = place_ends(jax.random.randint(splits[2], (TILES_ALL,), 0, IB_DEV), jax.random.fold_in(splits[2], 1), 0, IB_DEV - 1).astype(jnp.int32)
    tile1_owner_keys = jax.random.split(jax.random.fold_in(splits[3], 1), TILES_ALL // TILES1)
    tile1_owner_turns = jax.random.permutation(jax.random.fold_in(splits[3], 3), TILES_ALL // TILES1)
    tile1_owner = jax.vmap(lambda own, number: assign_block(jax.random.fold_in(splits[3], 2), own, number, TILES1, N_WIDE, 1, CAP, 2))(tile1_owner_keys, tile1_owner_turns).reshape((TILES_ALL, 1))
    tile1_slot = place_ends(jax.random.randint(splits[4], (TILES_ALL,), 0, BB_DEV), jax.random.fold_in(splits[4], 1), 0, BB_DEV - 1).astype(jnp.int32)
    tile2_values = normal_values(splits[5], (TILES_ALL, TILE, TILE), (TILE * TILES1 * N_NARROW // UGRP) ** -0.5, 0.3125, ((0, 32),))
    tile2_source = place_ends(jax.random.randint(splits[6], (TILES_ALL,), 0, BB_DEV), jax.random.fold_in(splits[6], 1), 0, BB_DEV - 1).astype(jnp.int32)
    tile2_owner_keys = jax.random.split(jax.random.fold_in(splits[7], 1), TILES_ALL // TILES1)
    tile2_owner_turns = jax.random.permutation(jax.random.fold_in(splits[7], 3), TILES_ALL // TILES1)
    tile2_owner = jax.vmap(lambda own, number: assign_block(jax.random.fold_in(splits[7], 2), own, number, TILES1, N_WIDE, 1, CAP, 2))(tile2_owner_keys, tile2_owner_turns).reshape((TILES_ALL, 1))
    tile2_slot = place_ends(jax.random.randint(splits[8], (TILES_ALL,), 0, UGRP), jax.random.fold_in(splits[8], 1), 0, UGRP - 1).astype(jnp.int32)
    weight = normal_values(splits[9], (F, F), F ** -0.5, 0.375)
    bundle_degree = place_ends(jax.random.randint(splits[10], (BUNDLES,), 1, 5), jax.random.fold_in(splits[10], 1), 1, 4).astype(jnp.int32)
    user_degree = place_ends(jax.random.randint(splits[11], (USERS,), 1, 5), jax.random.fold_in(splits[11], 1), 1, 4).astype(jnp.int32)
    cotangent = normal_values(splits[12], (USERS, F), 1.0, 6.0, ((0, 8),))
    return dict(items=items, tile1_values=tile1_values, tile1_source=tile1_source, tile1_owner=tile1_owner, tile1_slot=tile1_slot, tile2_values=tile2_values, tile2_source=tile2_source, tile2_owner=tile2_owner, tile2_slot=tile2_slot, weight=weight, bundle_degree=bundle_degree, user_degree=user_degree, cotangent=cotangent)


def spread(values, blocks, take, put, count, flip):
    vals = values.reshape(DEVICES, TILES1, TILE, TILE)
    take = take.reshape(DEVICES, TILES1).astype(jnp.int32)
    put = put.reshape(DEVICES, TILES1).astype(jnp.int32)
    form = "tji,tjf->tif" if flip else "tij,tjf->tif"

    def step(acc, inputs):
        tiles, taken, placed = inputs
        source = blocks[taken].astype(jnp.float32)
        product = jnp.einsum(form, tiles.astype(jnp.float32), source)
        product = lax.optimization_barrier(product.astype(jnp.bfloat16)).astype(jnp.float32)
        return acc.at[placed].add(product), None

    acc, _ = lax.scan(step, jnp.zeros((count, TILE, F), jnp.float32), (vals, take, put))
    return acc.reshape(count * TILE, F)


def reference(items, tile1_values, tile1_source, tile1_owner, tile1_slot, tile2_values, tile2_source, tile2_owner, tile2_slot, weight, bundle_degree, user_degree, cotangent):
    device = jnp.arange(TILES_ALL, dtype=jnp.int32) // TILES1
    narrow_of = device % N_NARROW
    source1 = device * IB_DEV + tile1_source
    target1 = (tile1_owner[:, 0] * N_NARROW + narrow_of) * BB_DEV + tile1_slot
    summed = spread(tile1_values, items.reshape(-1, TILE, F), source1, target1, BUNDLES // TILE, False)
    bundle_emb = (summed / bundle_degree[:, None].astype(jnp.float32)).astype(jnp.bfloat16)
    mixed = jnp.dot(bundle_emb, weight, preferred_element_type=jnp.float32)
    activated = jax.nn.silu(mixed).astype(jnp.bfloat16)
    source2 = device * BB_DEV + tile2_source
    target2 = tile2_owner[:, 0] * UGRP + tile2_slot
    gathered = spread(tile2_values, activated.reshape(-1, TILE, F), source2, target2, USERS // TILE, False)
    user_out = (gathered / user_degree[:, None].astype(jnp.float32)).astype(jnp.bfloat16)
    scaled_grad = (cotangent.astype(jnp.float32) / user_degree[:, None].astype(jnp.float32)).astype(jnp.bfloat16)
    grad_act = spread(tile2_values, scaled_grad.reshape(-1, TILE, F), target2, source2, BUNDLES // TILE, True)
    sigma = jax.nn.sigmoid(mixed)
    grad_mixed = (grad_act * sigma * (1.0 + mixed * (1.0 - sigma))).astype(jnp.bfloat16)
    grad_weight = jnp.dot(bundle_emb.T, grad_mixed, preferred_element_type=jnp.float32)
    grad_bundle = jnp.dot(grad_mixed, weight.T, preferred_element_type=jnp.float32).astype(jnp.bfloat16)
    return user_out, grad_weight, grad_bundle
```

```python
import functools

import jax
import jax.numpy as jnp
from jax import lax
from jax.experimental import pallas as pl
from jax.experimental.pallas import tpu as pltpu
from jax.sharding import PartitionSpec as P

F = 256
TILE = 128
CAP = 2
MESH = pl.DeviceIdType.MESH
f32 = jnp.float32
bf16 = jnp.bfloat16


def plan_kernel(width, tiles1, tiles2, owner1, slot1, owner2, slot2, table, count):
    size = width * CAP

    def clear(i, _):
        table[i] = 0
        table[size + i] = 0
        table[2 * size + i] = -1
        table[3 * size + i] = -1
        return 0

    lax.fori_loop(0, size, clear, 0)

    def reset(i, _):
        count[i] = 0
        return 0

    lax.fori_loop(0, 2 * width, reset, 0)

    def first(t, _):
        owner = owner1[t]
        place = owner * CAP + count[owner]
        count[owner] = count[owner] + 1
        table[place] = t
        table[2 * size + place] = slot1[t]
        return 0

    lax.fori_loop(0, tiles1, first, 0)

    def second(t, _):
        owner = owner2[t]
        place = owner * CAP + count[width + owner]
        count[width + owner] = count[width + owner] + 1
        table[size + place] = t
        table[3 * size + place] = slot2[t]
        table[4 * size + t] = place
        return 0

    lax.fori_loop(0, tiles2, second, 0)


def main_kernel(
    W, N, G, B, U, T2,
    table, source1, source2,
    items, tile1, tile2, weight, bdeg, udeg, cot,
    uout, gw_out, gb_out,
    labs, rlab, slab,
    send_a, send_c, recv_a, recv_b, recv_c,
    inv_u, scaled, acc1, emb, mixed, act, acc2, gact,
    gw_send, gw_recv, gw_part, gw_parts, gw_fin,
    red_send, red_recv,
    lab_s, lab_r, copy_sem, a_s, a_r, b_s, b_r, c_s, c_r,
    g1_s, g1_r, g2_s, g2_r, g3_s, g3_r, n_s, n_r,
):
    w = lax.axis_index("wide")
    n = lax.axis_index("narrow")
    H = W // G
    R = F // G
    SZ = W * CAP
    h, g = w // G, w % G

    def up(d):
        return lax.rem(w + d, W)

    def down(d):
        return lax.rem(w - d + W, W)

    def crossing(q):
        other = lax.rem(h * N + n + q, H * N)
        return (other // N) * G + g, other % N

    barrier = pltpu.get_barrier_semaphore()

    def greet(d, _):
        pl.semaphore_signal(barrier, inc=1, device_id=(up(d), n), device_id_type=MESH)
        return 0

    lax.fori_loop(1, W, greet, 0)

    def greet_cross(q, _):
        pl.semaphore_signal(barrier, inc=1, device_id=crossing(q), device_id_type=MESH)
        return 0

    lax.fori_loop(1, H * N, greet_cross, 0)
    if H > 1:
        def greet_group(d, _):
            peer = h * G + lax.rem(g + d, G)
            pl.semaphore_signal(barrier, inc=1, device_id=(peer, n), device_id_type=MESH)
            return 0

        lax.fori_loop(1, G, greet_group, 0)
    lane = lax.broadcasted_iota(jnp.int32, (8, 128), 1)

    def pack(o, _):
        v = jnp.zeros((8, 128), jnp.int32)
        for k in range(CAP):
            v = jnp.where(lane == k, table[2 * SZ + o * CAP + k], v)
            v = jnp.where(lane == CAP + k, table[3 * SZ + o * CAP + k], v)
        labs[o] = v
        return 0

    lax.fori_loop(0, W, pack, 0)
    rlab[w] = labs[w]
    pl.semaphore_wait(barrier, W - 1 + H * N - 1 + (G - 1 if H > 1 else 0))

    def remote(src, dst, ss, rs, dev):
        return pltpu.make_async_remote_copy(
            src_ref=src, dst_ref=dst, send_sem=ss, recv_sem=rs, device_id=dev, device_id_type=MESH
        )

    def wide_copy(src, dst, ss, rs, d):
        return remote(src.at[up(d)], dst.at[w], ss.at[d], rs.at[d], (up(d), n))

    def send_labels(d, _):
        wide_copy(labs, rlab, lab_s, lab_r, d).start()
        return 0

    lax.fori_loop(1, W, send_labels, 0)

    def term1(o, k):
        t = table[o * CAP + k]
        return jnp.dot(tile1[t], items[source1[t]], preferred_element_type=f32).astype(bf16)

    def send_terms1(d, _):
        o = up(d)
        for k in range(CAP):
            send_a[o, k] = term1(o, k)
        wide_copy(send_a, recv_a, a_s, a_r, d).start()
        return 0

    lax.fori_loop(1, W, send_terms1, 0)
    for k in range(CAP):
        recv_a[w, k] = term1(w, k)

    def scale(b, _):
        row = 1.0 / udeg[b].astype(f32)
        inv = jnp.transpose(jnp.broadcast_to(row, (TILE, TILE)))
        inv_u[b] = inv
        for c in range(F // TILE):
            cols = slice(c * TILE, (c + 1) * TILE)
            scaled[b, :, cols] = (cot[b, :, cols].astype(f32) * inv).astype(bf16)
        return 0

    lax.fori_loop(0, U, scale, 0)

    def wait_labels(d, _):
        c = wide_copy(labs, rlab, lab_s, lab_r, d)
        c.wait_send()
        c.wait_recv()
        return 0

    lax.fori_loop(1, W, wait_labels, 0)
    local = pltpu.make_async_copy(rlab, slab, copy_sem)
    local.start()
    local.wait()

    def wanted(o, k):
        return scaled[jnp.maximum(slab[o, 0, CAP + k], 0)]

    def send_replies(d, _):
        o = up(d)
        for k in range(CAP):
            send_c[o, k] = wanted(o, k)
        wide_copy(send_c, recv_c, c_s, c_r, d).start()
        return 0

    lax.fori_loop(1, W, send_replies, 0)
    for k in range(CAP):
        recv_c[w, k] = wanted(w, k)

    ROWS = 32

    def add_blocks(acc, recv, o, column, blocks):
        labels = [slab[o, 0, column + k] for k in range(CAP)]

        def part(r, _):
            rows = pl.ds(pl.multiple_of(r * ROWS, ROWS), ROWS)
            xs = [recv[o, k, rows, :].astype(f32) for k in range(CAP)]
            for b in range(blocks):
                total = acc[b, rows, :]
                for k in range(CAP):
                    total = total + xs[k] * (labels[k] == b).astype(f32)
                acc[b, rows, :] = total
            return 0

        lax.fori_loop(0, TILE // ROWS, part, 0)

    acc1[...] = jnp.zeros_like(acc1)
    add_blocks(acc1, recv_a, w, 0, B)

    def collect1(d, _):
        wide_copy(send_a, recv_a, a_s, a_r, d).wait_recv()
        add_blocks(acc1, recv_a, down(d), 0, B)
        return 0

    lax.fori_loop(1, W, collect1, 0)

    def transform(b, _):
        row = 1.0 / bdeg[b].astype(f32)
        inv = jnp.transpose(jnp.broadcast_to(row, (TILE, TILE)))
        for c in range(F // TILE):
            cols = slice(c * TILE, (c + 1) * TILE)
            emb[b, :, cols] = (acc1[b, :, cols] * inv).astype(bf16)
        m = jnp.dot(emb[b], weight[...], preferred_element_type=f32)
        mixed[b] = m
        act[b] = (m / (1.0 + jnp.exp(-m))).astype(bf16)
        return 0

    lax.fori_loop(0, B, transform, 0)

    def term2(o, k):
        t = table[SZ + o * CAP + k]
        return jnp.dot(tile2[t], act[source2[t]], preferred_element_type=f32).astype(bf16)

    def free_a(d, _):
        wide_copy(send_a, recv_a, a_s, a_r, d).wait_send()
        return 0

    lax.fori_loop(1, W, free_a, 0)

    def send_terms2(d, _):
        o = up(d)
        for k in range(CAP):
            send_a[o, k] = term2(o, k)
        wide_copy(send_a, recv_b, b_s, b_r, d).start()
        return 0

    lax.fori_loop(1, W, send_terms2, 0)
    for k in range(CAP):
        recv_b[w, k] = term2(w, k)

    def wait_replies(d, _):
        c = wide_copy(send_c, recv_c, c_s, c_r, d)
        c.wait_recv()
        c.wait_send()
        return 0

    acc2[...] = jnp.zeros_like(acc2)
    add_blocks(acc2, recv_b, w, CAP, U)
    gact[...] = jnp.zeros_like(gact)
    lax.fori_loop(1, W, wait_replies, 0)

    def back(t, _):
        place = table[4 * SZ + t]
        block = recv_c[place // CAP, place % CAP]
        x = lax.dot_general(
            tile2[t], block, (((0,), (0,)), ((), ())), preferred_element_type=f32
        )
        x = x.astype(bf16).astype(f32)
        for b in range(B):
            gact[b] += x * (source2[t] == b).astype(f32)
        return 0

    lax.fori_loop(0, T2, back, 0)

    def finish(b, total):
        m = mixed[b]
        s = 1.0 / (1.0 + jnp.exp(-m))
        gm = (gact[b] * s * (1.0 + m * (1.0 - s))).astype(bf16)
        gb_out[b] = lax.dot_general(
            gm, weight[...], (((1,), (1,)), ((), ())), preferred_element_type=f32
        ).astype(bf16)
        gw_out[...] += lax.dot_general(
            emb[b], gm, (((0,), (0,)), ((), ())), preferred_element_type=f32
        )
        return total

    gw_out[...] = jnp.zeros_like(gw_out)
    lax.fori_loop(0, B, finish, 0)

    for i in range(G):
        gw_send[i] = gw_out[i * R:(i + 1) * R, :].astype(bf16)

    def group(d):
        return lax.rem(g + d, G)

    def group_copy1(d):
        return remote(
            gw_send.at[group(d)], gw_recv.at[g], g1_s.at[d], g1_r.at[d], (h * G + group(d), n)
        )

    def cross_copy(q):
        return remote(gw_part, gw_parts.at[h * N + n], g2_s.at[q], g2_r.at[q], crossing(q))

    def group_copy3(d):
        return remote(
            gw_fin.at[g], gw_fin.at[g], g3_s.at[d], g3_r.at[d], (h * G + group(d), n)
        )

    def start_all(copy, size):
        def go(d, _):
            copy(d).start()
            return 0

        lax.fori_loop(1, size, go, 0)

    def wait_all(copy, size):
        def go(d, _):
            c = copy(d)
            c.wait_recv()
            c.wait_send()
            return 0

        lax.fori_loop(1, size, go, 0)

    start_all(group_copy1, G)
    gw_recv[g] = gw_send[g]

    def collect2(d, _):
        wide_copy(send_a, recv_b, b_s, b_r, d).wait_recv()
        add_blocks(acc2, recv_b, down(d), CAP, U)
        return 0

    half = W // 2
    lax.fori_loop(1, half, collect2, 0)
    wait_all(group_copy1, G)
    part = gw_recv[0].astype(f32)
    for i in range(1, G):
        part = part + gw_recv[i].astype(f32)
    gw_part[...] = part
    gw_parts[h * N + n] = part
    start_all(cross_copy, H * N)
    lax.fori_loop(half, W, collect2, 0)
    wait_all(cross_copy, H * N)
    part = gw_parts[0]
    for i in range(1, H * N):
        part = part + gw_parts[i]
    gw_fin[g] = part.astype(bf16)
    start_all(group_copy3, G)

    def free_b(d, _):
        wide_copy(send_a, recv_b, b_s, b_r, d).wait_send()
        return 0

    bits = N.bit_length() - 1
    size, base = U, 0
    spans = []
    for i in range(bits):
        size //= 2
        bit = (n // (1 << i)) % 2
        peer = n + (1 - 2 * bit) * (1 << i)
        mine, theirs = base + bit * size, base + (1 - bit) * size

        def ready(j, _, theirs=theirs):
            red_send[theirs + j] = acc2[theirs + j].astype(bf16)
            return 0

        lax.fori_loop(0, size, ready, 0)
        first = U - 2 * size
        c = remote(
            red_send.at[pl.ds(theirs, size)], red_recv.at[pl.ds(first, size)],
            n_s.at[i], n_r.at[i], (w, peer),
        )
        c.start()
        c.wait_recv()
        c.wait_send()

        def add(j, _, mine=mine, first=first):
            acc2[mine + j] += red_recv[first + j].astype(f32)
            return 0

        lax.fori_loop(0, size, add, 0)
        spans.append((mine, size, peer))
        base = mine

    def divide(j, _):
        b = base + j
        for c in range(F // TILE):
            cols = slice(c * TILE, (c + 1) * TILE)
            uout[b, :, cols] = (acc2[b, :, cols] * inv_u[b]).astype(bf16)
        return 0

    lax.fori_loop(0, size, divide, 0)
    for i, (mine, size, peer) in reversed(list(enumerate(spans))):
        span = uout.at[pl.ds(mine, size)]
        c = remote(span, span, n_s.at[bits + i], n_r.at[bits + i], (w, peer))
        c.start()
        c.wait_recv()
        c.wait_send()

    lax.fori_loop(1, W, free_b, 0)
    wait_all(group_copy3, G)
    for i in range(G):
        gw_out[i * R:(i + 1) * R, :] = gw_fin[i].astype(f32)


def local(
    items, tile1_values, tile1_source, tile1_owner, tile1_slot,
    tile2_values, tile2_source, tile2_owner, tile2_slot,
    weight, bundle_degree, user_degree, cotangent,
):
    W, N = lax.axis_size("wide"), lax.axis_size("narrow")
    G = min(W, 8)
    H = W // G
    B, U = bundle_degree.shape[0] // TILE, user_degree.shape[0] // TILE
    T1, T2 = tile1_values.shape[0], tile2_values.shape[0]
    R = F // G
    smem = pl.BlockSpec(memory_space=pltpu.SMEM)
    vmem = pl.BlockSpec(memory_space=pltpu.VMEM)
    table = pl.pallas_call(
        functools.partial(plan_kernel, W, T1, T2),
        out_shape=jax.ShapeDtypeStruct((4 * W * CAP + T2,), jnp.int32),
        in_specs=[smem] * 4,
        out_specs=smem,
        scratch_shapes=[pltpu.SMEM((2 * W,), jnp.int32)],
        name="plan",
    )(tile1_owner.reshape(-1), tile1_slot, tile2_owner.reshape(-1), tile2_slot)
    dma = pltpu.SemaphoreType.DMA
    bits = N.bit_length() - 1
    slots = (W, CAP, TILE, F)
    uout, gw, gb = pl.pallas_call(
        functools.partial(main_kernel, W, N, G, B, U, T2),
        out_shape=(
            jax.ShapeDtypeStruct((U, TILE, F), bf16),
            jax.ShapeDtypeStruct((F, F), f32),
            jax.ShapeDtypeStruct((B, TILE, F), bf16),
        ),
        in_specs=[smem] * 3 + [vmem] * 7,
        out_specs=(vmem,) * 3,
        scratch_shapes=[
            pltpu.VMEM((W, 8, 128), jnp.int32),
            pltpu.VMEM((W, 8, 128), jnp.int32),
            pltpu.SMEM((W, 8, 128), jnp.int32),
            pltpu.VMEM(slots, bf16),
            pltpu.VMEM(slots, bf16),
            pltpu.VMEM(slots, bf16),
            pltpu.VMEM(slots, bf16),
            pltpu.VMEM(slots, bf16),
            pltpu.VMEM((U, TILE, TILE), f32),
            pltpu.VMEM((U, TILE, F), bf16),
            pltpu.VMEM((B, TILE, F), f32),
            pltpu.VMEM((B, TILE, F), bf16),
            pltpu.VMEM((B, TILE, F), f32),
            pltpu.VMEM((B, TILE, F), bf16),
            pltpu.VMEM((U, TILE, F), f32),
            pltpu.VMEM((B, TILE, F), f32),
            pltpu.VMEM((G, R, F), bf16),
            pltpu.VMEM((G, R, F), bf16),
            pltpu.VMEM((R, F), f32),
            pltpu.VMEM((H * N, R, F), f32),
            pltpu.VMEM((G, R, F), bf16),
            pltpu.VMEM((U, TILE, F), bf16),
            pltpu.VMEM((U, TILE, F), bf16),
            dma((W,)), dma((W,)), dma,
            dma((W,)), dma((W,)), dma((W,)), dma((W,)), dma((W,)), dma((W,)),
            dma((G,)), dma((G,)), dma((H * N,)), dma((H * N,)), dma((G,)), dma((G,)),
            dma((2 * bits,)), dma((2 * bits,)),
        ],
        compiler_params=pltpu.CompilerParams(
            collective_id=0, has_side_effects=True, vmem_limit_bytes=60 * 1024 * 1024
        ),
        name="hypergraph",
    )(
        table, tile1_source, tile2_source,
        items.reshape(-1, TILE, F), tile1_values, tile2_values, weight,
        bundle_degree.reshape(B, 1, TILE), user_degree.reshape(U, 1, TILE),
        cotangent.reshape(U, TILE, F),
    )
    return uout.reshape(U * TILE, F), gw, gb.reshape(B * TILE, F)


def solution(mesh):
    both = ("wide", "narrow")
    in_specs = (
        P(both, None), P(both, None, None), P(both), P(both, None), P(both),
        P(both, None, None), P(both), P(both, None), P(both),
        P(), P(both), P("wide"), P("wide", None),
    )
    out_specs = (P("wide", None), P(), P(both, None))
    return jax.shard_map(local, mesh=mesh, in_specs=in_specs, out_specs=out_specs, check_vma=False)
```

```python
import functools

import jax
import jax.numpy as jnp
from jax import lax
from jax.experimental import pallas as pl
from jax.experimental.pallas import tpu as pltpu
from jax.sharding import PartitionSpec as P

F = 256
TILE = 128
CAP = 2
MESH = pl.DeviceIdType.MESH
f32 = jnp.float32
bf16 = jnp.bfloat16


def plan_kernel(width, tiles1, tiles2, owner1, slot1, owner2, slot2, table, count):
    size = width * CAP

    def clear(i, _):
        table[i] = 0
        table[size + i] = 0
        table[2 * size + i] = -1
        table[3 * size + i] = -1
        return 0

    lax.fori_loop(0, size, clear, 0)

    def reset(i, _):
        count[i] = 0
        return 0

    lax.fori_loop(0, 2 * width, reset, 0)

    def first(t, _):
        owner = owner1[t]
        place = owner * CAP + count[owner]
        count[owner] = count[owner] + 1
        table[place] = t
        table[2 * size + place] = slot1[t]
        return 0

    lax.fori_loop(0, tiles1, first, 0)

    def second(t, _):
        owner = owner2[t]
        place = owner * CAP + count[width + owner]
        count[width + owner] = count[width + owner] + 1
        table[size + place] = t
        table[3 * size + place] = slot2[t]
        table[4 * size + t] = place
        return 0

    lax.fori_loop(0, tiles2, second, 0)


def main_kernel(
    W, N, G, B, U, T2,
    table, source1, source2,
    items, tile1, tile2, weight, bdeg, udeg, cot,
    uout, gw_out, gb_out,
    labs, rlab, slab,
    send_a, send_c, recv_a, recv_b, recv_c,
    inv_u, scaled, relay, half_send, half_recv, acc1, gact, emb, mixed, act, acc2,
    gw_send, gw_recv, gw_part, gw_parts, gw_fin,
    red_send, red_recv,
    lab_s, lab_r, copy_sem, a_s, a_r, b_s, b_r, c_s, c_r,
    g1_s, g1_r, g2_s, g2_r, g3_s, g3_r, n_s, n_r, r_s, r_r, h_s, h_r,
):
    w = lax.axis_index("wide")
    n = lax.axis_index("narrow")
    H = W // G
    R = F // G
    SZ = W * CAP
    h, g = w // G, w % G
    Q = W // 2
    side, place_in = w // Q, w % Q
    pair = lax.rem(w + Q, W)
    C = F // TILE
    bits = N.bit_length() - 1

    def up(d):
        return lax.rem(w + d, W)

    def down(d):
        return lax.rem(w - d + W, W)

    def crossing(q):
        other = lax.rem(h * N + n + q, H * N)
        return (other // N) * G + g, other % N

    barrier = pltpu.get_barrier_semaphore()

    def greet(d, _):
        pl.semaphore_signal(barrier, inc=1, device_id=(up(d), n), device_id_type=MESH)
        return 0

    lax.fori_loop(1, W, greet, 0)

    def greet_cross(q, _):
        pl.semaphore_signal(barrier, inc=1, device_id=crossing(q), device_id_type=MESH)
        return 0

    lax.fori_loop(1, H * N, greet_cross, 0)
    if H > 1:
        def greet_group(d, _):
            peer = h * G + lax.rem(g + d, G)
            pl.semaphore_signal(barrier, inc=1, device_id=(peer, n), device_id_type=MESH)
            return 0

        lax.fori_loop(1, G, greet_group, 0)
    lane = lax.broadcasted_iota(jnp.int32, (8, 128), 1)

    def pack(o, _):
        v = jnp.zeros((8, 128), jnp.int32)
        for k in range(CAP):
            v = jnp.where(lane == k, table[2 * SZ + o * CAP + k], v)
            v = jnp.where(lane == CAP + k, table[3 * SZ + o * CAP + k], v)
            far = lax.rem(o + Q, W) * CAP + k
            v = jnp.where(lane == 2 * CAP + k, table[2 * SZ + far], v)
            v = jnp.where(lane == 3 * CAP + k, table[3 * SZ + far], v)
        labs[o] = v
        return 0

    lax.fori_loop(0, W, pack, 0)
    rlab[w] = labs[w]
    pl.semaphore_wait(barrier, W - 1 + H * N - 1 + (G - 1 if H > 1 else 0))

    def remote(src, dst, ss, rs, dev):
        return pltpu.make_async_remote_copy(
            src_ref=src, dst_ref=dst, send_sem=ss, recv_sem=rs, device_id=dev, device_id_type=MESH
        )

    def wide_copy(src, dst, ss, rs, d):
        return remote(src.at[up(d)], dst.at[w], ss.at[d], rs.at[d], (up(d), n))

    def send_labels(d, _):
        wide_copy(labs, rlab, lab_s, lab_r, d).start()
        return 0

    lax.fori_loop(1, W, send_labels, 0)

    spans = []
    size, base = U, 0
    for i in range(bits):
        size //= 2
        bit = (n // (1 << i)) % 2
        peer = n + (1 - 2 * bit) * (1 << i)
        spans.append((base + bit * size, base + (1 - bit) * size, size, peer))
        base = base + bit * size

    def scale(b):
        row = 1.0 / udeg[b].astype(f32)
        inv = jnp.transpose(jnp.broadcast_to(row, (TILE, TILE)))
        inv_u[b] = inv
        for c in range(C):
            cols = slice(c * TILE, (c + 1) * TILE)
            scaled[b, :, cols] = (cot[b, :, cols].astype(f32) * inv).astype(bf16)

    def scale_first(j, _):
        scale(base + j)
        return 0

    def scale_rest(j, _):
        scale(lax.rem(base + j, U))
        return 0

    lax.fori_loop(0, size, scale_first, 0)
    over = remote(
        scaled.at[pl.ds(base, size)], relay.at[pl.ds(base, size)], h_s.at[0], h_r.at[0], (pair, n)
    )
    over.start()

    def mate(d):
        return side * Q + lax.rem(place_in + d, Q)

    def mate_back(d):
        return side * Q + lax.rem(place_in - d + Q, Q)

    def far(o):
        return lax.rem(o + Q, W)

    def near_copy(src, dst, ss, rs, d):
        return remote(src.at[mate(d)], dst.at[w], ss.at[d], rs.at[d], (mate(d), n))

    def far_copy(src, dst, ss, rs, d):
        return remote(src.at[far(mate(d))], dst.at[pair], ss.at[Q + d], rs.at[Q + d], (mate(d), n))

    def term1(o, k):
        t = table[o * CAP + k]
        return jnp.dot(tile1[t], items[source1[t]], preferred_element_type=f32).astype(bf16)

    def send_far1(d, _):
        o = far(mate(d))
        for k in range(CAP):
            send_a[o, k] = term1(o, k)
        far_copy(send_a, recv_a, a_s, a_r, d).start()
        return 0

    def send_near1(d, _):
        o = mate(d)
        for k in range(CAP):
            send_a[o, k] = term1(o, k)
        near_copy(send_a, recv_a, a_s, a_r, d).start()
        return 0

    lax.fori_loop(1, Q, send_far1, 0)
    lax.fori_loop(1, Q, send_near1, 0)
    for k in range(CAP):
        recv_a[pair, k] = term1(pair, k)
        recv_a[w, k] = term1(w, k)
    lax.fori_loop(size, U, scale_rest, 0)

    def wait_labels(d, _):
        c = wide_copy(labs, rlab, lab_s, lab_r, d)
        c.wait_send()
        c.wait_recv()
        return 0

    lax.fori_loop(1, W, wait_labels, 0)
    local = pltpu.make_async_copy(rlab, slab, copy_sem)
    local.start()
    local.wait()

    ROWS = 32

    def add_blocks(acc, recv, place, o, column, blocks, cols):
        labels = [slab[o, 0, column + k] for k in range(CAP)]

        def part(r, _):
            rows = pl.ds(pl.multiple_of(r * ROWS, ROWS), ROWS)
            xs = [recv[place, k, rows, cols].astype(f32) for k in range(CAP)]
            for b in range(blocks):
                total = acc[b, rows, cols]
                for k in range(CAP):
                    total = total + xs[k] * (labels[k] == b).astype(f32)
                acc[b, rows, cols] = total
            return 0

        lax.fori_loop(0, TILE // ROWS, part, 0)

    every = slice(0, F)
    gact[...] = jnp.zeros_like(gact)
    add_blocks(gact, recv_a, pair, w, 2 * CAP, B, every)

    def collect_far(d, _):
        far_copy(send_a, recv_a, a_s, a_r, d).wait_recv()
        o = mate_back(d)
        add_blocks(gact, recv_a, far(o), o, 2 * CAP, B, every)
        return 0

    lax.fori_loop(1, Q, collect_far, 0)
    half_send[...] = gact[...].astype(bf16)
    across = remote(half_send, half_recv, h_s.at[1], h_r.at[1], (pair, n))
    across.start()

    def near_block(o, k):
        return scaled[jnp.maximum(slab[o, 0, CAP + k], 0)]

    def far_block(o, k):
        return relay[jnp.maximum(slab[o, 0, 3 * CAP + k], 0)]

    def send_near_replies(d, _):
        o = mate(d)
        for k in range(CAP):
            send_c[o, k] = near_block(o, k)
        near_copy(send_c, recv_c, c_s, c_r, d).start()
        return 0

    def send_far_replies(d, _):
        o = mate(d)
        for k in range(CAP):
            send_c[far(o), k] = far_block(o, k)
        far_copy(send_c, recv_c, c_s, c_r, d).start()
        return 0

    def relay_copy(i):
        mine, _, many, peer = spans[i]
        span = relay.at[pl.ds(mine, many)]
        return remote(span, span, r_s.at[i], r_r.at[i], (w, peer))

    over.wait_recv()
    relay_copy(bits - 1).start()
    lax.fori_loop(1, Q, send_near_replies, 0)
    for k in range(CAP):
        recv_c[w, k] = near_block(w, k)

    acc1[...] = jnp.zeros_like(acc1)
    add_blocks(acc1, recv_a, w, w, 0, B, every)

    def collect_near(d, _):
        near_copy(send_a, recv_a, a_s, a_r, d).wait_recv()
        o = mate_back(d)
        add_blocks(acc1, recv_a, o, o, 0, B, every)
        return 0

    for i in range(bits - 1, -1, -1):
        relay_copy(i).wait_recv()
        relay_copy(i).wait_send()
        if i > 0:
            relay_copy(i - 1).start()
        if i == bits - 1:
            lax.fori_loop(1, Q, collect_near, 0)
    lax.fori_loop(1, Q, send_far_replies, 0)
    for k in range(CAP):
        recv_c[pair, k] = far_block(w, k)
    across.wait_recv()
    acc1[...] += half_recv[...].astype(f32)

    def transform(b, _):
        row = 1.0 / bdeg[b].astype(f32)
        inv = jnp.transpose(jnp.broadcast_to(row, (TILE, TILE)))
        for c in range(F // TILE):
            cols = slice(c * TILE, (c + 1) * TILE)
            emb[b, :, cols] = (acc1[b, :, cols] * inv).astype(bf16)
        m = jnp.dot(emb[b], weight[...], preferred_element_type=f32)
        mixed[b] = m
        act[b] = (m / (1.0 + jnp.exp(-m))).astype(bf16)
        return 0

    lax.fori_loop(0, B, transform, 0)

    def term2(o, k):
        t = table[SZ + o * CAP + k]
        return jnp.dot(tile2[t], act[source2[t]], preferred_element_type=f32).astype(bf16)

    def free_a(d, _):
        near_copy(send_a, recv_a, a_s, a_r, d).wait_send()
        far_copy(send_a, recv_a, a_s, a_r, d).wait_send()
        return 0

    lax.fori_loop(1, Q, free_a, 0)

    def column(c):
        return slice(c * TILE, (c + 1) * TILE)

    def user_copy(c, d):
        return remote(
            send_a.at[up(d), :, :, column(c)], recv_b.at[w, :, :, column(c)],
            b_s.at[c, d], b_r.at[c, d], (up(d), n),
        )

    def send_terms2(d, _):
        o = up(d)
        for k in range(CAP):
            send_a[o, k] = term2(o, k)
        user_copy(0, d).start()
        return 0

    lax.fori_loop(1, W, send_terms2, 0)
    for k in range(CAP):
        recv_b[w, k] = term2(w, k)

    def wait_replies(d, _):
        for c in (near_copy(send_c, recv_c, c_s, c_r, d), far_copy(send_c, recv_c, c_s, c_r, d)):
            c.wait_recv()
            c.wait_send()
        return 0

    acc2[...] = jnp.zeros_like(acc2)
    add_blocks(acc2, recv_b, w, w, CAP, U, every)
    gact[...] = jnp.zeros_like(gact)
    lax.fori_loop(1, Q, wait_replies, 0)

    def back(t, _):
        place = table[4 * SZ + t]
        block = recv_c[place // CAP, place % CAP]
        x = lax.dot_general(
            tile2[t], block, (((0,), (0,)), ((), ())), preferred_element_type=f32
        )
        x = x.astype(bf16).astype(f32)
        for b in range(B):
            gact[b] += x * (source2[t] == b).astype(f32)
        return 0

    lax.fori_loop(0, T2, back, 0)

    def send_later(d, _):
        user_copy(0, d).wait_send()
        for c in range(1, C):
            user_copy(c, d).start()
        return 0

    lax.fori_loop(1, W, send_later, 0)

    def finish(b, total):
        m = mixed[b]
        s = 1.0 / (1.0 + jnp.exp(-m))
        gm = (gact[b] * s * (1.0 + m * (1.0 - s))).astype(bf16)
        gb_out[b] = lax.dot_general(
            gm, weight[...], (((1,), (1,)), ((), ())), preferred_element_type=f32
        ).astype(bf16)
        gw_out[...] += lax.dot_general(
            emb[b], gm, (((0,), (0,)), ((), ())), preferred_element_type=f32
        )
        return total

    gw_out[...] = jnp.zeros_like(gw_out)
    lax.fori_loop(0, B, finish, 0)

    for i in range(G):
        gw_send[i] = gw_out[i * R:(i + 1) * R, :].astype(bf16)

    def group(d):
        return lax.rem(g + d, G)

    def group_copy1(d):
        return remote(
            gw_send.at[group(d)], gw_recv.at[g], g1_s.at[d], g1_r.at[d], (h * G + group(d), n)
        )

    def cross_copy(q):
        return remote(gw_part, gw_parts.at[h * N + n], g2_s.at[q], g2_r.at[q], crossing(q))

    def group_copy3(d):
        return remote(
            gw_fin.at[g], gw_fin.at[g], g3_s.at[d], g3_r.at[d], (h * G + group(d), n)
        )

    def start_all(copy, size):
        def go(d, _):
            copy(d).start()
            return 0

        lax.fori_loop(1, size, go, 0)

    def wait_all(copy, size):
        def go(d, _):
            c = copy(d)
            c.wait_recv()
            c.wait_send()
            return 0

        lax.fori_loop(1, size, go, 0)

    start_all(group_copy1, G)
    gw_recv[g] = gw_send[g]

    def collect2(c):
        def go(d, _):
            user_copy(c, d).wait_recv()
            add_blocks(acc2, recv_b, down(d), down(d), CAP, U, column(c))
            return 0

        return go

    def halve_copy(c, i):
        _, theirs, many, peer = spans[i]
        return remote(
            red_send.at[c, pl.ds(theirs, many)], red_recv.at[c, pl.ds(U - 2 * many, many)],
            n_s.at[c, i], n_r.at[c, i], (w, peer),
        )

    def double_copy(c, i):
        mine, _, many, peer = spans[i]
        span = uout.at[pl.ds(mine, many), :, column(c)]
        return remote(span, span, n_s.at[c, bits + i], n_r.at[c, bits + i], (w, peer))

    def halve_start(c, i):
        _, theirs, many, _ = spans[i]

        def ready(j, _):
            red_send[c, theirs + j] = acc2[theirs + j, :, column(c)].astype(bf16)
            return 0

        lax.fori_loop(0, many, ready, 0)
        halve_copy(c, i).start()

    def halve_end(c, i):
        mine, _, many, _ = spans[i]
        x = halve_copy(c, i)
        x.wait_recv()
        x.wait_send()

        def add(j, _):
            acc2[mine + j, :, column(c)] += red_recv[c, U - 2 * many + j].astype(f32)
            return 0

        lax.fori_loop(0, many, add, 0)

    def divide(c):
        def go(j, _):
            b = base + j
            uout[b, :, column(c)] = (acc2[b, :, column(c)] * inv_u[b]).astype(bf16)
            return 0

        lax.fori_loop(0, size, go, 0)

    def double_end(c, i):
        x = double_copy(c, i)
        x.wait_recv()
        x.wait_send()

    def narrow_step(c, step):
        if step < bits:
            if step > 0:
                halve_end(c, step - 1)
            halve_start(c, step)
        elif step < 2 * bits:
            i = 2 * bits - 1 - step
            if step == bits:
                halve_end(c, bits - 1)
                divide(c)
            else:
                double_end(c, i + 1)
            double_copy(c, i).start()
        else:
            double_end(c, 0)

    lax.fori_loop(1, W, collect2(0), 0)
    narrow_step(0, 0)
    wait_all(group_copy1, G)
    part = gw_recv[0].astype(f32)
    for i in range(1, G):
        part = part + gw_recv[i].astype(f32)
    gw_part[...] = part
    gw_parts[h * N + n] = part
    start_all(cross_copy, H * N)
    steps = 2 * bits
    for c in range(1, C):
        for step in range(1, steps + 1):
            narrow_step(c - 1, step)
            if step == 1 and c == 1:
                wait_all(cross_copy, H * N)
                part = gw_parts[0]
                for i in range(1, H * N):
                    part = part + gw_parts[i]
                gw_fin[g] = part.astype(bf16)
                start_all(group_copy3, G)
            lo = 1 + (W - 1) * (step - 1) // steps
            hi = 1 + (W - 1) * step // steps
            lax.fori_loop(lo, hi, collect2(c), 0)
        narrow_step(c, 0)
    for step in range(1, steps + 1):
        narrow_step(C - 1, step)

    def free_b(d, _):
        for c in range(1, C):
            user_copy(c, d).wait_send()
        return 0

    over.wait_send()
    across.wait_send()
    lax.fori_loop(1, W, free_b, 0)
    wait_all(group_copy3, G)
    for i in range(G):
        gw_out[i * R:(i + 1) * R, :] = gw_fin[i].astype(f32)


def local(
    items, tile1_values, tile1_source, tile1_owner, tile1_slot,
    tile2_values, tile2_source, tile2_owner, tile2_slot,
    weight, bundle_degree, user_degree, cotangent,
):
    W, N = lax.axis_size("wide"), lax.axis_size("narrow")
    G = min(W, 8)
    H = W // G
    B, U = bundle_degree.shape[0] // TILE, user_degree.shape[0] // TILE
    T1, T2 = tile1_values.shape[0], tile2_values.shape[0]
    R = F // G
    smem = pl.BlockSpec(memory_space=pltpu.SMEM)
    vmem = pl.BlockSpec(memory_space=pltpu.VMEM)
    table = pl.pallas_call(
        functools.partial(plan_kernel, W, T1, T2),
        out_shape=jax.ShapeDtypeStruct((4 * W * CAP + T2,), jnp.int32),
        in_specs=[smem] * 4,
        out_specs=smem,
        scratch_shapes=[pltpu.SMEM((2 * W,), jnp.int32)],
        name="plan",
    )(tile1_owner.reshape(-1), tile1_slot, tile2_owner.reshape(-1), tile2_slot)
    dma = pltpu.SemaphoreType.DMA
    bits = N.bit_length() - 1
    slots = (W, CAP, TILE, F)
    uout, gw, gb = pl.pallas_call(
        functools.partial(main_kernel, W, N, G, B, U, T2),
        out_shape=(
            jax.ShapeDtypeStruct((U, TILE, F), bf16),
            jax.ShapeDtypeStruct((F, F), f32),
            jax.ShapeDtypeStruct((B, TILE, F), bf16),
        ),
        in_specs=[smem] * 3 + [vmem] * 7,
        out_specs=(vmem,) * 3,
        scratch_shapes=[
            pltpu.VMEM((W, 8, 128), jnp.int32),
            pltpu.VMEM((W, 8, 128), jnp.int32),
            pltpu.SMEM((W, 8, 128), jnp.int32),
            pltpu.VMEM(slots, bf16),
            pltpu.VMEM(slots, bf16),
            pltpu.VMEM(slots, bf16),
            pltpu.VMEM(slots, bf16),
            pltpu.VMEM(slots, bf16),
            pltpu.VMEM((U, TILE, TILE), f32),
            pltpu.VMEM((U, TILE, F), bf16),
            pltpu.VMEM((U, TILE, F), bf16),
            pltpu.VMEM((B, TILE, F), bf16),
            pltpu.VMEM((B, TILE, F), bf16),
            pltpu.VMEM((B, TILE, F), f32),
            pltpu.VMEM((B, TILE, F), f32),
            pltpu.VMEM((B, TILE, F), bf16),
            pltpu.VMEM((B, TILE, F), f32),
            pltpu.VMEM((B, TILE, F), bf16),
            pltpu.VMEM((U, TILE, F), f32),
            pltpu.VMEM((G, R, F), bf16),
            pltpu.VMEM((G, R, F), bf16),
            pltpu.VMEM((R, F), f32),
            pltpu.VMEM((H * N, R, F), f32),
            pltpu.VMEM((G, R, F), bf16),
            pltpu.VMEM((F // TILE, U, TILE, TILE), bf16),
            pltpu.VMEM((F // TILE, U, TILE, TILE), bf16),
            dma((W,)), dma((W,)), dma,
            dma((W,)), dma((W,)), dma((F // TILE, W)), dma((F // TILE, W)), dma((W,)), dma((W,)),
            dma((G,)), dma((G,)), dma((H * N,)), dma((H * N,)), dma((G,)), dma((G,)),
            dma((F // TILE, 2 * bits)), dma((F // TILE, 2 * bits)), dma((bits,)), dma((bits,)),
            dma((2,)), dma((2,)),
        ],
        compiler_params=pltpu.CompilerParams(
            collective_id=0, has_side_effects=True, vmem_limit_bytes=61 * 1024 * 1024
        ),
        name="hypergraph",
    )(
        table, tile1_source, tile2_source,
        items.reshape(-1, TILE, F), tile1_values, tile2_values, weight,
        bundle_degree.reshape(B, 1, TILE), user_degree.reshape(U, 1, TILE),
        cotangent.reshape(U, TILE, F),
    )
    return uout.reshape(U * TILE, F), gw, gb.reshape(B * TILE, F)


def solution(mesh):
    both = ("wide", "narrow")
    in_specs = (
        P(both, None), P(both, None, None), P(both), P(both, None), P(both),
        P(both, None, None), P(both), P(both, None), P(both),
        P(), P(both), P("wide"), P("wide", None),
    )
    out_specs = (P("wide", None), P(), P(both, None))
    return jax.shard_map(local, mesh=mesh, in_specs=in_specs, out_specs=out_specs, check_vma=False)
```

```python
import functools

import jax
import jax.numpy as jnp
from jax import lax
from jax.experimental import pallas as pl
from jax.experimental.pallas import tpu as pltpu
from jax.sharding import PartitionSpec as P

F = 256
TILE = 128
CAP = 2
MESH = pl.DeviceIdType.MESH
f32 = jnp.float32
bf16 = jnp.bfloat16


def plan_kernel(width, tiles1, tiles2, owner1, slot1, owner2, slot2, table, count):
    size = width * CAP

    def clear(i, _):
        table[i] = 0
        table[size + i] = 0
        table[2 * size + i] = -1
        table[3 * size + i] = -1
        return 0

    lax.fori_loop(0, size, clear, 0)

    def reset(i, _):
        count[i] = 0
        return 0

    lax.fori_loop(0, 2 * width, reset, 0)

    def first(t, _):
        owner = owner1[t]
        place = owner * CAP + count[owner]
        count[owner] = count[owner] + 1
        table[place] = t
        table[2 * size + place] = slot1[t]
        return 0

    lax.fori_loop(0, tiles1, first, 0)

    def second(t, _):
        owner = owner2[t]
        place = owner * CAP + count[width + owner]
        count[width + owner] = count[width + owner] + 1
        table[size + place] = t
        table[3 * size + place] = slot2[t]
        table[4 * size + t] = place
        return 0

    lax.fori_loop(0, tiles2, second, 0)


def main_kernel(
    W, N, G, B, U, T2,
    table, source1, source2,
    items, tile1, tile2, weight, bdeg, udeg, cot,
    uout, gw_out, gb_out,
    labs, rlab, slab,
    send_a, send_c, recv_a, recv_b, recv_c,
    inv_u, scaled, relay, half_send, half_recv, acc1, gact, emb, mixed, act, acc2,
    gw_send, gw_recv, gw_part, gw_parts, gw_fin,
    red_send, red_recv,
    lab_s, lab_r, copy_sem, a_s, a_r, b_s, b_r, c_s, c_r,
    g1_s, g1_r, g2_s, g2_r, g3_s, g3_r, n_s, n_r, r_s, r_r, h_s, h_r,
):
    w = lax.axis_index("wide")
    n = lax.axis_index("narrow")
    H = W // G
    R = F // G
    SZ = W * CAP
    h, g = w // G, w % G
    Q = W // 2
    side, place_in = w // Q, w % Q
    pair = lax.rem(w + Q, W)
    C = F // TILE
    bits = N.bit_length() - 1

    def up(d):
        return lax.rem(w + d, W)

    def down(d):
        return lax.rem(w - d + W, W)

    def crossing(q):
        other = lax.rem(h * N + n + q, H * N)
        return (other // N) * G + g, other % N

    barrier = pltpu.get_barrier_semaphore()

    def greet(d, _):
        pl.semaphore_signal(barrier, inc=1, device_id=(up(d), n), device_id_type=MESH)
        return 0

    lax.fori_loop(1, W, greet, 0)

    def greet_cross(q, _):
        pl.semaphore_signal(barrier, inc=1, device_id=crossing(q), device_id_type=MESH)
        return 0

    lax.fori_loop(1, H * N, greet_cross, 0)
    if H > 1:
        def greet_group(d, _):
            peer = h * G + lax.rem(g + d, G)
            pl.semaphore_signal(barrier, inc=1, device_id=(peer, n), device_id_type=MESH)
            return 0

        lax.fori_loop(1, G, greet_group, 0)
    lane = lax.broadcasted_iota(jnp.int32, (8, 128), 1)

    def pack(o, _):
        v = jnp.zeros((8, 128), jnp.int32)
        for k in range(CAP):
            v = jnp.where(lane == k, table[2 * SZ + o * CAP + k], v)
            v = jnp.where(lane == CAP + k, table[3 * SZ + o * CAP + k], v)
            far = lax.rem(o + Q, W) * CAP + k
            v = jnp.where(lane == 2 * CAP + k, table[2 * SZ + far], v)
            v = jnp.where(lane == 3 * CAP + k, table[3 * SZ + far], v)
        labs[o] = v
        return 0

    lax.fori_loop(0, W, pack, 0)
    rlab[w] = labs[w]
    pl.semaphore_wait(barrier, W - 1 + H * N - 1 + (G - 1 if H > 1 else 0))

    def remote(src, dst, ss, rs, dev):
        return pltpu.make_async_remote_copy(
            src_ref=src, dst_ref=dst, send_sem=ss, recv_sem=rs, device_id=dev, device_id_type=MESH
        )

    def wide_copy(src, dst, ss, rs, d):
        return remote(src.at[up(d)], dst.at[w], ss.at[d], rs.at[d], (up(d), n))

    def send_labels(d, _):
        wide_copy(labs, rlab, lab_s, lab_r, d).start()
        return 0

    lax.fori_loop(1, W, send_labels, 0)

    spans = []
    size, base = U, 0
    for i in range(bits):
        size //= 2
        bit = (n // (1 << i)) % 2
        peer = n + (1 - 2 * bit) * (1 << i)
        spans.append((base + bit * size, base + (1 - bit) * size, size, peer))
        base = base + bit * size

    def scale(b):
        row = 1.0 / udeg[b].astype(f32)
        inv = jnp.transpose(jnp.broadcast_to(row, (TILE, TILE)))
        inv_u[b] = inv
        for c in range(C):
            cols = slice(c * TILE, (c + 1) * TILE)
            scaled[b, :, cols] = (cot[b, :, cols].astype(f32) * inv).astype(bf16)

    def scale_first(j, _):
        scale(base + j)
        return 0

    def scale_rest(j, _):
        scale(lax.rem(base + j, U))
        return 0

    lax.fori_loop(0, size, scale_first, 0)
    over = remote(
        scaled.at[pl.ds(base, size)], relay.at[pl.ds(base, size)], h_s.at[0], h_r.at[0], (pair, n)
    )
    over.start()

    def mate(d):
        return side * Q + lax.rem(place_in + d, Q)

    def mate_back(d):
        return side * Q + lax.rem(place_in - d + Q, Q)

    def far(o):
        return lax.rem(o + Q, W)

    def near_copy(src, dst, ss, rs, d):
        return remote(src.at[mate(d)], dst.at[w], ss.at[d], rs.at[d], (mate(d), n))

    def far_copy(src, dst, ss, rs, d):
        return remote(src.at[far(mate(d))], dst.at[pair], ss.at[Q + d], rs.at[Q + d], (mate(d), n))

    def term1(o, k):
        t = table[o * CAP + k]
        return jnp.dot(tile1[t], items[source1[t]], preferred_element_type=f32).astype(bf16)

    def send_far1(d, _):
        o = far(mate(d))
        for k in range(CAP):
            send_a[o, k] = term1(o, k)
        far_copy(send_a, recv_a, a_s, a_r, d).start()
        return 0

    def make_near1(d, _):
        o = mate(d)
        for k in range(CAP):
            send_a[o, k] = term1(o, k)
        return 0

    lax.fori_loop(1, Q, send_far1, 0)
    lax.fori_loop(1, Q, make_near1, 0)
    for k in range(CAP):
        recv_a[pair, k] = term1(pair, k)
        recv_a[w, k] = term1(w, k)
    lax.fori_loop(size, U, scale_rest, 0)

    def release_near1(d, _):
        far_copy(send_a, recv_a, a_s, a_r, d).wait_send()
        near_copy(send_a, recv_a, a_s, a_r, d).start()
        return 0

    lax.fori_loop(1, Q, release_near1, 0)

    def wait_labels(d, _):
        c = wide_copy(labs, rlab, lab_s, lab_r, d)
        c.wait_send()
        c.wait_recv()
        return 0

    lax.fori_loop(1, W, wait_labels, 0)
    local = pltpu.make_async_copy(rlab.at[:, pl.ds(0, 1), :], slab, copy_sem)
    local.start()
    local.wait()

    ROWS = 32

    def add_blocks(acc, recv, place, o, column, blocks, cols):
        labels = [slab[o, 0, column + k] for k in range(CAP)]

        def part(r, _):
            rows = pl.ds(pl.multiple_of(r * ROWS, ROWS), ROWS)
            xs = [recv[place, k, rows, cols].astype(f32) for k in range(CAP)]
            for b in range(blocks):
                total = acc[b, rows, cols]
                for k in range(CAP):
                    total = total + xs[k] * (labels[k] == b).astype(f32)
                acc[b, rows, cols] = total
            return 0

        lax.fori_loop(0, TILE // ROWS, part, 0)

    every = slice(0, F)
    gact[...] = jnp.zeros_like(gact)
    add_blocks(gact, recv_a, pair, w, 2 * CAP, B, every)

    def collect_far(d, _):
        far_copy(send_a, recv_a, a_s, a_r, d).wait_recv()
        o = mate_back(d)
        add_blocks(gact, recv_a, far(o), o, 2 * CAP, B, every)
        return 0

    lax.fori_loop(1, Q, collect_far, 0)
    half_send[...] = gact[...].astype(bf16)
    across = remote(half_send, half_recv, h_s.at[1], h_r.at[1], (pair, n))
    across.start()

    def near_block(o, k):
        return scaled[jnp.maximum(slab[o, 0, CAP + k], 0)]

    def far_block(o, k):
        return relay[jnp.maximum(slab[o, 0, 3 * CAP + k], 0)]

    def send_near_replies(d, _):
        o = mate(d)
        for k in range(CAP):
            send_c[o, k] = near_block(o, k)
        near_copy(send_c, recv_c, c_s, c_r, d).start()
        return 0

    def send_far_replies(d, _):
        o = mate(d)
        for k in range(CAP):
            send_c[far(o), k] = far_block(o, k)
        far_copy(send_c, recv_c, c_s, c_r, d).start()
        return 0

    def relay_copy(i):
        mine, _, many, peer = spans[i]
        span = relay.at[pl.ds(mine, many)]
        return remote(span, span, r_s.at[i], r_r.at[i], (w, peer))

    over.wait_recv()
    relay_copy(bits - 1).start()
    lax.fori_loop(1, Q, send_near_replies, 0)
    for k in range(CAP):
        recv_c[w, k] = near_block(w, k)

    acc1[...] = jnp.zeros_like(acc1)
    add_blocks(acc1, recv_a, w, w, 0, B, every)

    def collect_near(d, _):
        near_copy(send_a, recv_a, a_s, a_r, d).wait_recv()
        o = mate_back(d)
        add_blocks(acc1, recv_a, o, o, 0, B, every)
        return 0

    lax.fori_loop(1, Q, collect_near, 0)
    for i in range(bits - 1, 0, -1):
        relay_copy(i).wait_recv()
        relay_copy(i).wait_send()
        relay_copy(i - 1).start()
    across.wait_recv()
    acc1[...] += half_recv[...].astype(f32)

    def transform(b, _):
        row = 1.0 / bdeg[b].astype(f32)
        inv = jnp.transpose(jnp.broadcast_to(row, (TILE, TILE)))
        for c in range(F // TILE):
            cols = slice(c * TILE, (c + 1) * TILE)
            emb[b, :, cols] = (acc1[b, :, cols] * inv).astype(bf16)
        m = jnp.dot(emb[b], weight[...], preferred_element_type=f32)
        mixed[b] = m
        act[b] = (m / (1.0 + jnp.exp(-m))).astype(bf16)
        return 0

    lax.fori_loop(0, B, transform, 0)

    def term2(o, k):
        t = table[SZ + o * CAP + k]
        return jnp.dot(tile2[t], act[source2[t]], preferred_element_type=f32).astype(bf16)

    def free_a(d, _):
        near_copy(send_a, recv_a, a_s, a_r, d).wait_send()
        return 0

    lax.fori_loop(1, Q, free_a, 0)

    def column(c):
        return slice(c * TILE, (c + 1) * TILE)

    def user_copy(c, d):
        return remote(
            send_a.at[up(d), :, :, column(c)], recv_b.at[w, :, :, column(c)],
            b_s.at[c, d], b_r.at[c, d], (up(d), n),
        )

    def send_terms2(d, _):
        o = up(d)
        for k in range(CAP):
            send_a[o, k] = term2(o, k)
        user_copy(0, d).start()
        return 0

    lax.fori_loop(1, W, send_terms2, 0)
    for k in range(CAP):
        recv_b[w, k] = term2(w, k)

    relay_copy(0).wait_recv()
    relay_copy(0).wait_send()
    lax.fori_loop(1, Q, send_far_replies, 0)
    for k in range(CAP):
        recv_c[pair, k] = far_block(w, k)

    def send_later(d, _):
        user_copy(0, d).wait_send()
        for c in range(1, C):
            user_copy(c, d).start()
        return 0

    lax.fori_loop(1, W, send_later, 0)

    def wait_replies(d, _):
        for c in (near_copy(send_c, recv_c, c_s, c_r, d), far_copy(send_c, recv_c, c_s, c_r, d)):
            c.wait_recv()
            c.wait_send()
        return 0

    acc2[...] = jnp.zeros_like(acc2)
    add_blocks(acc2, recv_b, w, w, CAP, U, every)
    gact[...] = jnp.zeros_like(gact)
    lax.fori_loop(1, Q, wait_replies, 0)

    def back(t, _):
        place = table[4 * SZ + t]
        block = recv_c[place // CAP, place % CAP]
        x = lax.dot_general(
            tile2[t], block, (((0,), (0,)), ((), ())), preferred_element_type=f32
        )
        x = x.astype(bf16).astype(f32)
        for b in range(B):
            gact[b] += x * (source2[t] == b).astype(f32)
        return 0

    lax.fori_loop(0, T2, back, 0)

    def group(d):
        return lax.rem(g + d, G)

    def group_copy1(d):
        return remote(
            gw_send.at[group(d)], gw_recv.at[g], g1_s.at[d], g1_r.at[d], (h * G + group(d), n)
        )

    def cross_copy(q):
        return remote(gw_part, gw_parts.at[h * N + n], g2_s.at[q], g2_r.at[q], crossing(q))

    def group_copy3(d):
        return remote(
            gw_fin.at[g], gw_fin.at[g], g3_s.at[d], g3_r.at[d], (h * G + group(d), n)
        )

    def start_all(copy, size):
        def go(d, _):
            copy(d).start()
            return 0

        lax.fori_loop(1, size, go, 0)

    def wait_all(copy, size):
        def go(d, _):
            c = copy(d)
            c.wait_recv()
            c.wait_send()
            return 0

        lax.fori_loop(1, size, go, 0)

    def collect2(c):
        def go(d, _):
            user_copy(c, d).wait_recv()
            add_blocks(acc2, recv_b, down(d), down(d), CAP, U, column(c))
            return 0

        return go

    def halve_copy(c, i):
        _, theirs, many, peer = spans[i]
        return remote(
            red_send.at[c, pl.ds(theirs, many)], red_recv.at[c, pl.ds(U - 2 * many, many)],
            n_s.at[c, i], n_r.at[c, i], (w, peer),
        )

    def double_copy(c, i):
        mine, _, many, peer = spans[i]
        span = uout.at[pl.ds(mine, many), :, column(c)]
        return remote(span, span, n_s.at[c, bits + i], n_r.at[c, bits + i], (w, peer))

    def halve_start(c, i):
        _, theirs, many, _ = spans[i]

        def ready(j, _):
            red_send[c, theirs + j] = acc2[theirs + j, :, column(c)].astype(bf16)
            return 0

        lax.fori_loop(0, many, ready, 0)
        halve_copy(c, i).start()

    def halve_end(c, i):
        mine, _, many, _ = spans[i]
        x = halve_copy(c, i)
        x.wait_recv()
        x.wait_send()

        def add(j, _):
            acc2[mine + j, :, column(c)] += red_recv[c, U - 2 * many + j].astype(f32)
            return 0

        lax.fori_loop(0, many, add, 0)

    def divide(c):
        def go(j, _):
            b = base + j
            uout[b, :, column(c)] = (acc2[b, :, column(c)] * inv_u[b]).astype(bf16)
            return 0

        lax.fori_loop(0, size, go, 0)

    def double_end(c, i):
        x = double_copy(c, i)
        x.wait_recv()
        x.wait_send()

    def narrow_step(c, step):
        if step < bits:
            if step > 0:
                halve_end(c, step - 1)
            halve_start(c, step)
        elif step < 2 * bits:
            i = 2 * bits - 1 - step
            if step == bits:
                halve_end(c, bits - 1)
                divide(c)
            else:
                double_end(c, i + 1)
            double_copy(c, i).start()
        else:
            double_end(c, 0)

    lax.fori_loop(1, W, collect2(0), 0)
    narrow_step(0, 0)
    def finish(b, total):
        m = mixed[b]
        s = 1.0 / (1.0 + jnp.exp(-m))
        gm = (gact[b] * s * (1.0 + m * (1.0 - s))).astype(bf16)
        gb_out[b] = lax.dot_general(
            gm, weight[...], (((1,), (1,)), ((), ())), preferred_element_type=f32
        ).astype(bf16)
        gw_out[...] += lax.dot_general(
            emb[b], gm, (((0,), (0,)), ((), ())), preferred_element_type=f32
        )
        return total

    gw_out[...] = jnp.zeros_like(gw_out)
    lax.fori_loop(0, B, finish, 0)

    for i in range(G):
        gw_send[i] = gw_out[i * R:(i + 1) * R, :].astype(bf16)

    start_all(group_copy1, G)
    gw_recv[g] = gw_send[g]
    steps = 2 * bits
    narrow_step(0, 1)
    wait_all(group_copy1, G)
    part = gw_recv[0].astype(f32)
    for i in range(1, G):
        part = part + gw_recv[i].astype(f32)
    gw_part[...] = part
    gw_parts[h * N + n] = part
    start_all(cross_copy, H * N)
    for c in range(1, C):
        for step in range(1, steps + 1):
            if step > 1 or c > 1:
                narrow_step(c - 1, step)
            if step == 2 and c == 1:
                wait_all(cross_copy, H * N)
                part = gw_parts[0]
                for i in range(1, H * N):
                    part = part + gw_parts[i]
                gw_fin[g] = part.astype(bf16)
                start_all(group_copy3, G)
            lo = 1 + (W - 1) * (step - 1) // steps
            hi = 1 + (W - 1) * step // steps
            lax.fori_loop(lo, hi, collect2(c), 0)
        narrow_step(c, 0)
    for step in range(1, steps + 1):
        narrow_step(C - 1, step)

    def free_b(d, _):
        for c in range(1, C):
            user_copy(c, d).wait_send()
        return 0

    over.wait_send()
    across.wait_send()
    lax.fori_loop(1, W, free_b, 0)
    wait_all(group_copy3, G)
    for i in range(G):
        gw_out[i * R:(i + 1) * R, :] = gw_fin[i].astype(f32)


def place_kernel(a, b, c, x, y, z, sems):
    copies = [pltpu.make_async_copy(src, dst, sems.at[i]) for i, (src, dst) in enumerate(
        [(a, x), (b, y), (c, z)]
    )]
    for copy in copies:
        copy.start()
    for copy in copies:
        copy.wait()


def local(
    items, tile1_values, tile1_source, tile1_owner, tile1_slot,
    tile2_values, tile2_source, tile2_owner, tile2_slot,
    weight, bundle_degree, user_degree, cotangent,
):
    W, N = lax.axis_size("wide"), lax.axis_size("narrow")
    G = min(W, 8)
    H = W // G
    B, U = bundle_degree.shape[0] // TILE, user_degree.shape[0] // TILE
    T1, T2 = tile1_values.shape[0], tile2_values.shape[0]
    R = F // G
    smem = pl.BlockSpec(memory_space=pltpu.SMEM)
    vmem = pl.BlockSpec(memory_space=pltpu.VMEM)
    table = pl.pallas_call(
        functools.partial(plan_kernel, W, T1, T2),
        out_shape=jax.ShapeDtypeStruct((4 * W * CAP + T2,), jnp.int32),
        in_specs=[smem] * 4,
        out_specs=smem,
        scratch_shapes=[pltpu.SMEM((2 * W,), jnp.int32)],
        name="plan",
    )(tile1_owner.reshape(-1), tile1_slot, tile2_owner.reshape(-1), tile2_slot)
    dma = pltpu.SemaphoreType.DMA
    bits = N.bit_length() - 1
    slots = (W, CAP, TILE, F)
    uout, gw, gb = pl.pallas_call(
        functools.partial(main_kernel, W, N, G, B, U, T2),
        out_shape=(
            jax.ShapeDtypeStruct((U, TILE, F), bf16),
            jax.ShapeDtypeStruct((F, F), f32),
            jax.ShapeDtypeStruct((B, TILE, F), bf16),
        ),
        in_specs=[smem] * 3 + [vmem] * 7,
        out_specs=(vmem,) * 3,
        scratch_shapes=[
            pltpu.VMEM((W, 8, 128), jnp.int32),
            pltpu.VMEM((W, 8, 128), jnp.int32),
            pltpu.SMEM((W, 1, 128), jnp.int32),
            pltpu.VMEM(slots, bf16),
            pltpu.VMEM(slots, bf16),
            pltpu.VMEM(slots, bf16),
            pltpu.VMEM(slots, bf16),
            pltpu.VMEM(slots, bf16),
            pltpu.VMEM((U, TILE, TILE), f32),
            pltpu.VMEM((U, TILE, F), bf16),
            pltpu.VMEM((U, TILE, F), bf16),
            pltpu.VMEM((B, TILE, F), bf16),
            pltpu.VMEM((B, TILE, F), bf16),
            pltpu.VMEM((B, TILE, F), f32),
            pltpu.VMEM((B, TILE, F), f32),
            pltpu.VMEM((B, TILE, F), bf16),
            pltpu.VMEM((B, TILE, F), f32),
            pltpu.VMEM((B, TILE, F), bf16),
            pltpu.VMEM((U, TILE, F), f32),
            pltpu.VMEM((G, R, F), bf16),
            pltpu.VMEM((G, R, F), bf16),
            pltpu.VMEM((R, F), f32),
            pltpu.VMEM((H * N, R, F), f32),
            pltpu.VMEM((G, R, F), bf16),
            pltpu.VMEM((F // TILE, U, TILE, TILE), bf16),
            pltpu.VMEM((F // TILE, U, TILE, TILE), bf16),
            dma((W,)), dma((W,)), dma,
            dma((W,)), dma((W,)), dma((F // TILE, W)), dma((F // TILE, W)), dma((W,)), dma((W,)),
            dma((G,)), dma((G,)), dma((H * N,)), dma((H * N,)), dma((G,)), dma((G,)),
            dma((F // TILE, 2 * bits)), dma((F // TILE, 2 * bits)), dma((bits,)), dma((bits,)),
            dma((2,)), dma((2,)),
        ],
        compiler_params=pltpu.CompilerParams(
            collective_id=0, has_side_effects=True, vmem_limit_bytes=61 * 1024 * 1024
        ),
        name="hypergraph",
    )(
        table, tile1_source, tile2_source,
        items.reshape(-1, TILE, F), tile1_values, tile2_values, weight,
        bundle_degree.reshape(B, 1, TILE), user_degree.reshape(U, 1, TILE),
        cotangent.reshape(U, TILE, F),
    )
    hbm = pl.BlockSpec(memory_space=pl.ANY)
    uout, gw, gb = pl.pallas_call(
        place_kernel,
        out_shape=tuple(jax.ShapeDtypeStruct(x.shape, x.dtype) for x in (uout, gw, gb)),
        in_specs=[hbm] * 3,
        out_specs=(hbm,) * 3,
        scratch_shapes=[dma((3,))],
        name="place",
    )(uout, gw, gb)
    return uout.reshape(U * TILE, F), gw, gb.reshape(B * TILE, F)


def solution(mesh):
    both = ("wide", "narrow")
    in_specs = (
        P(both, None), P(both, None, None), P(both), P(both, None), P(both),
        P(both, None, None), P(both), P(both, None), P(both),
        P(), P(both), P("wide"), P("wide", None),
    )
    out_specs = (P("wide", None), P(), P(both, None))
    return jax.shard_map(local, mesh=mesh, in_specs=in_specs, out_specs=out_specs, check_vma=False)
```

```python
import functools

import jax
import jax.numpy as jnp
from jax import lax
from jax.experimental import pallas as pl
from jax.experimental.pallas import tpu as pltpu
from jax.sharding import PartitionSpec as P

F = 256
TILE = 128
CAP = 2
MESH = pl.DeviceIdType.MESH
f32 = jnp.float32
bf16 = jnp.bfloat16


def plan_kernel(width, tiles1, tiles2, owner1, slot1, owner2, slot2, table, count):
    size = width * CAP

    def clear(i, _):
        table[i] = 0
        table[size + i] = 0
        table[2 * size + i] = -1
        table[3 * size + i] = -1
        return 0

    lax.fori_loop(0, size, clear, 0)

    def reset(i, _):
        count[i] = 0
        return 0

    lax.fori_loop(0, 2 * width, reset, 0)

    def first(t, _):
        owner = owner1[t]
        place = owner * CAP + count[owner]
        count[owner] = count[owner] + 1
        table[place] = t
        table[2 * size + place] = slot1[t]
        return 0

    lax.fori_loop(0, tiles1, first, 0)

    def second(t, _):
        owner = owner2[t]
        place = owner * CAP + count[width + owner]
        count[width + owner] = count[width + owner] + 1
        table[size + place] = t
        table[3 * size + place] = slot2[t]
        table[4 * size + t] = place
        return 0

    lax.fori_loop(0, tiles2, second, 0)


def main_kernel(
    W, N, G, B, U, T2,
    table, source1, source2,
    items, tile1, tile2, weight, bdeg, udeg, cot,
    users, gw_fin, gb_out,
    labs, rlab, slab,
    send_a, send_c, recv_a, recv_b, recv_c,
    inv_u, scaled, relay, half_send, half_recv, acc1, gact, emb, mixed, act, acc2,
    gw_out, gw_send, gw_recv, gw_part, gw_parts,
    red_send, red_recv,
    lab_s, lab_r, copy_sem, a_s, a_r, b_s, b_r, c_s, c_r,
    g1_s, g1_r, g2_s, g2_r, g3_s, g3_r, n_s, n_r, r_s, r_r, h_s, h_r,
):
    w = lax.axis_index("wide")
    n = lax.axis_index("narrow")
    H = W // G
    R = F // G
    SZ = W * CAP
    h, g = w // G, w % G
    Q = W // 2
    side, place_in = w // Q, w % Q
    pair = lax.rem(w + Q, W)
    C = F // TILE
    bits = N.bit_length() - 1

    def up(d):
        return lax.rem(w + d, W)

    def down(d):
        return lax.rem(w - d + W, W)

    def crossing(q):
        other = lax.rem(h * N + n + q, H * N)
        return (other // N) * G + g, other % N

    barrier = pltpu.get_barrier_semaphore()

    def greet(d, _):
        pl.semaphore_signal(barrier, inc=1, device_id=(up(d), n), device_id_type=MESH)
        return 0

    lax.fori_loop(1, W, greet, 0)

    def greet_cross(q, _):
        pl.semaphore_signal(barrier, inc=1, device_id=crossing(q), device_id_type=MESH)
        return 0

    lax.fori_loop(1, H * N, greet_cross, 0)
    if H > 1:
        def greet_group(d, _):
            peer = h * G + lax.rem(g + d, G)
            pl.semaphore_signal(barrier, inc=1, device_id=(peer, n), device_id_type=MESH)
            return 0

        lax.fori_loop(1, G, greet_group, 0)
    lane = lax.broadcasted_iota(jnp.int32, (8, 128), 1)

    def pack(o, _):
        v = jnp.zeros((8, 128), jnp.int32)
        for k in range(CAP):
            v = jnp.where(lane == k, table[2 * SZ + o * CAP + k], v)
            v = jnp.where(lane == CAP + k, table[3 * SZ + o * CAP + k], v)
            far = lax.rem(o + Q, W) * CAP + k
            v = jnp.where(lane == 2 * CAP + k, table[2 * SZ + far], v)
            v = jnp.where(lane == 3 * CAP + k, table[3 * SZ + far], v)
        labs[o] = v
        return 0

    lax.fori_loop(0, W, pack, 0)
    rlab[w] = labs[w]
    pl.semaphore_wait(barrier, W - 1 + H * N - 1 + (G - 1 if H > 1 else 0))

    def remote(src, dst, ss, rs, dev):
        return pltpu.make_async_remote_copy(
            src_ref=src, dst_ref=dst, send_sem=ss, recv_sem=rs, device_id=dev, device_id_type=MESH
        )

    def wide_copy(src, dst, ss, rs, d):
        return remote(src.at[up(d)], dst.at[w], ss.at[d], rs.at[d], (up(d), n))

    def send_labels(d, _):
        wide_copy(labs, rlab, lab_s, lab_r, d).start()
        return 0

    lax.fori_loop(1, W, send_labels, 0)

    spans = []
    size, base = U, 0
    for i in range(bits):
        size //= 2
        bit = (n // (1 << i)) % 2
        peer = n + (1 - 2 * bit) * (1 << i)
        spans.append((base + bit * size, base + (1 - bit) * size, size, peer))
        base = base + bit * size

    def scale(b):
        row = 1.0 / udeg[b].astype(f32)
        inv = jnp.transpose(jnp.broadcast_to(row, (TILE, TILE)))
        inv_u[b] = inv
        for c in range(C):
            cols = slice(c * TILE, (c + 1) * TILE)
            scaled[b, :, cols] = (cot[b, :, cols].astype(f32) * inv).astype(bf16)

    def scale_first(j, _):
        scale(base + j)
        return 0

    def scale_rest(j, _):
        scale(lax.rem(base + j, U))
        return 0

    lax.fori_loop(0, size, scale_first, 0)
    over = remote(
        scaled.at[pl.ds(base, size)], relay.at[pl.ds(base, size)], h_s.at[0], h_r.at[0], (pair, n)
    )
    over.start()

    def mate(d):
        return side * Q + lax.rem(place_in + d, Q)

    def mate_back(d):
        return side * Q + lax.rem(place_in - d + Q, Q)

    def far(o):
        return lax.rem(o + Q, W)

    def near_copy(src, dst, ss, rs, d):
        return remote(src.at[mate(d)], dst.at[w], ss.at[d], rs.at[d], (mate(d), n))

    def far_copy(src, dst, ss, rs, d):
        return remote(src.at[far(mate(d))], dst.at[pair], ss.at[Q + d], rs.at[Q + d], (mate(d), n))

    def term1(o, k):
        t = table[o * CAP + k]
        return jnp.dot(tile1[t], items[source1[t]], preferred_element_type=f32).astype(bf16)

    def put(buffer, o, k, value):
        for c in range(C):
            buffer[o, c, k] = value[:, c * TILE:(c + 1) * TILE]

    def send_far1(d, _):
        o = far(mate(d))
        for k in range(CAP):
            put(send_a, o, k, term1(o, k))
        far_copy(send_a, recv_a, a_s, a_r, d).start()
        return 0

    def make_near1(d, _):
        o = mate(d)
        for k in range(CAP):
            put(send_a, o, k, term1(o, k))
        return 0

    lax.fori_loop(1, Q, send_far1, 0)
    lax.fori_loop(1, Q, make_near1, 0)
    for k in range(CAP):
        put(recv_a, pair, k, term1(pair, k))
        put(recv_a, w, k, term1(w, k))
    lax.fori_loop(size, U, scale_rest, 0)

    def release_near1(d, _):
        far_copy(send_a, recv_a, a_s, a_r, d).wait_send()
        near_copy(send_a, recv_a, a_s, a_r, d).start()
        return 0

    lax.fori_loop(1, Q, release_near1, 0)

    def wait_labels(d, _):
        c = wide_copy(labs, rlab, lab_s, lab_r, d)
        c.wait_send()
        c.wait_recv()
        return 0

    lax.fori_loop(1, W, wait_labels, 0)
    local = pltpu.make_async_copy(rlab.at[:, pl.ds(0, 1), :], slab, copy_sem)
    local.start()
    local.wait()

    ROWS = 32

    def add_blocks(acc, recv, place, o, start, blocks, columns=range(C)):
        labels = [slab[o, 0, start + k] for k in range(CAP)]

        def part(r, _):
            rows = pl.ds(pl.multiple_of(r * ROWS, ROWS), ROWS)
            for c in columns:
                cols = slice(c * TILE, (c + 1) * TILE)
                xs = [recv[place, c, k, rows, :].astype(f32) for k in range(CAP)]
                for b in range(blocks):
                    total = acc[b, rows, cols]
                    for k in range(CAP):
                        total = total + xs[k] * (labels[k] == b).astype(f32)
                    acc[b, rows, cols] = total
            return 0

        lax.fori_loop(0, TILE // ROWS, part, 0)

    gact[...] = jnp.zeros_like(gact)
    add_blocks(gact, recv_a, pair, w, 2 * CAP, B)

    def collect_far(d, _):
        far_copy(send_a, recv_a, a_s, a_r, d).wait_recv()
        o = mate_back(d)
        add_blocks(gact, recv_a, far(o), o, 2 * CAP, B)
        return 0

    lax.fori_loop(1, Q, collect_far, 0)
    half_send[...] = gact[...].astype(bf16)
    across = remote(half_send, half_recv, h_s.at[1], h_r.at[1], (pair, n))
    across.start()

    def near_block(o, k):
        return scaled[jnp.maximum(slab[o, 0, CAP + k], 0)]

    def far_block(o, k):
        return relay[jnp.maximum(slab[o, 0, 3 * CAP + k], 0)]

    def send_near_replies(d, _):
        o = mate(d)
        for k in range(CAP):
            send_c[o, k] = near_block(o, k)
        near_copy(send_c, recv_c, c_s, c_r, d).start()
        return 0

    def send_far_replies(d, _):
        o = mate(d)
        for k in range(CAP):
            send_c[far(o), k] = far_block(o, k)
        far_copy(send_c, recv_c, c_s, c_r, d).start()
        return 0

    def relay_copy(i):
        mine, _, many, peer = spans[i]
        span = relay.at[pl.ds(mine, many)]
        return remote(span, span, r_s.at[i], r_r.at[i], (w, peer))

    over.wait_recv()
    relay_copy(bits - 1).start()
    lax.fori_loop(1, Q, send_near_replies, 0)
    for k in range(CAP):
        recv_c[w, k] = near_block(w, k)

    acc1[...] = jnp.zeros_like(acc1)
    add_blocks(acc1, recv_a, w, w, 0, B)

    def collect_near(d, _):
        near_copy(send_a, recv_a, a_s, a_r, d).wait_recv()
        o = mate_back(d)
        add_blocks(acc1, recv_a, o, o, 0, B)
        return 0

    lax.fori_loop(1, Q, collect_near, 0)
    for i in range(bits - 1, 0, -1):
        relay_copy(i).wait_recv()
        relay_copy(i).wait_send()
        relay_copy(i - 1).start()
    across.wait_recv()
    acc1[...] += half_recv[...].astype(f32)

    def transform(b, _):
        row = 1.0 / bdeg[b].astype(f32)
        inv = jnp.transpose(jnp.broadcast_to(row, (TILE, TILE)))
        for c in range(F // TILE):
            cols = slice(c * TILE, (c + 1) * TILE)
            emb[b, :, cols] = (acc1[b, :, cols] * inv).astype(bf16)
        m = jnp.dot(emb[b], weight[...], preferred_element_type=f32)
        mixed[b] = m
        act[b] = (m / (1.0 + jnp.exp(-m))).astype(bf16)
        return 0

    lax.fori_loop(0, B, transform, 0)

    def term2(o, k):
        t = table[SZ + o * CAP + k]
        return jnp.dot(tile2[t], act[source2[t]], preferred_element_type=f32).astype(bf16)

    def free_a(d, _):
        near_copy(send_a, recv_a, a_s, a_r, d).wait_send()
        return 0

    lax.fori_loop(1, Q, free_a, 0)

    def column(c):
        return slice(c * TILE, (c + 1) * TILE)

    def user_copy(c, d):
        return remote(
            send_a.at[up(d), c], recv_b.at[w, c],
            b_s.at[c, d], b_r.at[c, d], (up(d), n),
        )

    def send_terms2(d, _):
        o = up(d)
        for k in range(CAP):
            put(send_a, o, k, term2(o, k))
        user_copy(0, d).start()
        return 0

    lax.fori_loop(1, W, send_terms2, 0)
    for k in range(CAP):
        put(recv_b, w, k, term2(w, k))

    relay_copy(0).wait_recv()
    relay_copy(0).wait_send()
    lax.fori_loop(1, Q, send_far_replies, 0)
    for k in range(CAP):
        recv_c[pair, k] = far_block(w, k)

    def send_later(d, _):
        user_copy(0, d).wait_send()
        for c in range(1, C):
            user_copy(c, d).start()
        return 0

    lax.fori_loop(1, W, send_later, 0)

    def wait_replies(d, _):
        for c in (near_copy(send_c, recv_c, c_s, c_r, d), far_copy(send_c, recv_c, c_s, c_r, d)):
            c.wait_recv()
            c.wait_send()
        return 0

    acc2[...] = jnp.zeros_like(acc2)
    add_blocks(acc2, recv_b, w, w, CAP, U)
    gact[...] = jnp.zeros_like(gact)
    lax.fori_loop(1, Q, wait_replies, 0)

    def back(t, _):
        place = table[4 * SZ + t]
        block = recv_c[place // CAP, place % CAP]
        x = lax.dot_general(
            tile2[t], block, (((0,), (0,)), ((), ())), preferred_element_type=f32
        )
        x = x.astype(bf16).astype(f32)
        for b in range(B):
            gact[b] += x * (source2[t] == b).astype(f32)
        return 0

    lax.fori_loop(0, T2, back, 0)

    def group(d):
        return lax.rem(g + d, G)

    def group_copy1(d):
        return remote(
            gw_send.at[group(d)], gw_recv.at[g], g1_s.at[d], g1_r.at[d], (h * G + group(d), n)
        )

    def cross_copy(q):
        return remote(gw_part, gw_parts.at[h * N + n], g2_s.at[q], g2_r.at[q], crossing(q))

    def group_copy3(d):
        return remote(
            gw_fin.at[g], gw_fin.at[g], g3_s.at[d], g3_r.at[d], (h * G + group(d), n)
        )

    def start_all(copy, size):
        def go(d, _):
            copy(d).start()
            return 0

        lax.fori_loop(1, size, go, 0)

    def wait_all(copy, size):
        def go(d, _):
            c = copy(d)
            c.wait_recv()
            c.wait_send()
            return 0

        lax.fori_loop(1, size, go, 0)

    def collect2(c):
        def go(d, _):
            user_copy(c, d).wait_recv()
            add_blocks(acc2, recv_b, down(d), down(d), CAP, U, [c])
            return 0

        return go

    def halve_copy(c, i):
        _, theirs, many, peer = spans[i]
        return remote(
            red_send.at[c, pl.ds(theirs, many)], red_recv.at[c, pl.ds(U - 2 * many, many)],
            n_s.at[c, i], n_r.at[c, i], (w, peer),
        )

    def double_copy(c, i):
        mine, _, many, peer = spans[i]
        span = users.at[c, pl.ds(mine, many)]
        return remote(span, span, n_s.at[c, bits + i], n_r.at[c, bits + i], (w, peer))

    def halve_start(c, i):
        _, theirs, many, _ = spans[i]

        def ready(j, _):
            red_send[c, theirs + j] = acc2[theirs + j, :, column(c)].astype(bf16)
            return 0

        lax.fori_loop(0, many, ready, 0)
        halve_copy(c, i).start()

    def halve_end(c, i):
        mine, _, many, _ = spans[i]
        x = halve_copy(c, i)
        x.wait_recv()
        x.wait_send()

        def add(j, _):
            acc2[mine + j, :, column(c)] += red_recv[c, U - 2 * many + j].astype(f32)
            return 0

        lax.fori_loop(0, many, add, 0)

    def divide(c):
        def go(j, _):
            b = base + j
            users[c, b] = (acc2[b, :, column(c)] * inv_u[b]).astype(bf16)
            return 0

        lax.fori_loop(0, size, go, 0)

    def double_end(c, i):
        x = double_copy(c, i)
        x.wait_recv()
        x.wait_send()

    def narrow_step(c, step):
        if step < bits:
            if step > 0:
                halve_end(c, step - 1)
            halve_start(c, step)
        elif step < 2 * bits:
            i = 2 * bits - 1 - step
            if step == bits:
                halve_end(c, bits - 1)
                divide(c)
            else:
                double_end(c, i + 1)
            double_copy(c, i).start()
        else:
            double_end(c, 0)

    lax.fori_loop(1, W, collect2(0), 0)
    narrow_step(0, 0)
    def finish(b, total):
        m = mixed[b]
        s = 1.0 / (1.0 + jnp.exp(-m))
        gm = (gact[b] * s * (1.0 + m * (1.0 - s))).astype(bf16)
        gb_out[b] = lax.dot_general(
            gm, weight[...], (((1,), (1,)), ((), ())), preferred_element_type=f32
        ).astype(bf16)
        gw_out[...] += lax.dot_general(
            emb[b], gm, (((0,), (0,)), ((), ())), preferred_element_type=f32
        )
        return total

    gw_out[...] = jnp.zeros_like(gw_out)
    lax.fori_loop(0, B, finish, 0)

    for i in range(G):
        gw_send[i] = gw_out[i * R:(i + 1) * R, :].astype(bf16)

    start_all(group_copy1, G)
    gw_recv[g] = gw_send[g]
    steps = 2 * bits
    narrow_step(0, 1)
    wait_all(group_copy1, G)
    part = gw_recv[0].astype(f32)
    for i in range(1, G):
        part = part + gw_recv[i].astype(f32)
    gw_part[...] = part
    gw_parts[h * N + n] = part
    start_all(cross_copy, H * N)
    for c in range(1, C):
        for step in range(1, steps + 1):
            if step > 1 or c > 1:
                narrow_step(c - 1, step)
            if step == 2 and c == 1:
                wait_all(cross_copy, H * N)
                part = gw_parts[0]
                for i in range(1, H * N):
                    part = part + gw_parts[i]
                gw_fin[g] = part.astype(bf16)
                start_all(group_copy3, G)
            lo = 1 + (W - 1) * (step - 1) // steps
            hi = 1 + (W - 1) * step // steps
            lax.fori_loop(lo, hi, collect2(c), 0)
        narrow_step(c, 0)
    for step in range(1, steps + 1):
        narrow_step(C - 1, step)

    def free_b(d, _):
        for c in range(1, C):
            user_copy(c, d).wait_send()
        return 0

    over.wait_send()
    across.wait_send()
    lax.fori_loop(1, W, free_b, 0)
    wait_all(group_copy3, G)


def place_kernel(users, gw, gb, x, y, z):
    columns, blocks = users.shape[0], users.shape[1]
    rows = gw.shape[1]

    def block(b, _):
        for c in range(columns):
            x[b, :, c * TILE:(c + 1) * TILE] = users[c, b]
        return 0

    lax.fori_loop(0, blocks, block, 0)
    for i in range(gw.shape[0]):
        y[i * rows:(i + 1) * rows, :] = gw[i].astype(f32)
    z[...] = gb[...]


def local(
    items, tile1_values, tile1_source, tile1_owner, tile1_slot,
    tile2_values, tile2_source, tile2_owner, tile2_slot,
    weight, bundle_degree, user_degree, cotangent,
):
    W, N = lax.axis_size("wide"), lax.axis_size("narrow")
    G = min(W, 8)
    H = W // G
    B, U = bundle_degree.shape[0] // TILE, user_degree.shape[0] // TILE
    T1, T2 = tile1_values.shape[0], tile2_values.shape[0]
    R = F // G
    smem = pl.BlockSpec(memory_space=pltpu.SMEM)
    vmem = pl.BlockSpec(memory_space=pltpu.VMEM)
    table = pl.pallas_call(
        functools.partial(plan_kernel, W, T1, T2),
        out_shape=jax.ShapeDtypeStruct((4 * W * CAP + T2,), jnp.int32),
        in_specs=[smem] * 4,
        out_specs=smem,
        scratch_shapes=[pltpu.SMEM((2 * W,), jnp.int32)],
        name="plan",
    )(tile1_owner.reshape(-1), tile1_slot, tile2_owner.reshape(-1), tile2_slot)
    dma = pltpu.SemaphoreType.DMA
    bits = N.bit_length() - 1
    slots = (W, CAP, TILE, F)
    halves = (W, F // TILE, CAP, TILE, TILE)
    users, gw, gb = pl.pallas_call(
        functools.partial(main_kernel, W, N, G, B, U, T2),
        out_shape=(
            jax.ShapeDtypeStruct((F // TILE, U, TILE, TILE), bf16),
            jax.ShapeDtypeStruct((G, R, F), bf16),
            jax.ShapeDtypeStruct((B, TILE, F), bf16),
        ),
        in_specs=[smem] * 3 + [vmem] * 7,
        out_specs=(vmem,) * 3,
        scratch_shapes=[
            pltpu.VMEM((W, 8, 128), jnp.int32),
            pltpu.VMEM((W, 8, 128), jnp.int32),
            pltpu.SMEM((W, 1, 128), jnp.int32),
            pltpu.VMEM(halves, bf16),
            pltpu.VMEM(slots, bf16),
            pltpu.VMEM(halves, bf16),
            pltpu.VMEM(halves, bf16),
            pltpu.VMEM(slots, bf16),
            pltpu.VMEM((U, TILE, TILE), f32),
            pltpu.VMEM((U, TILE, F), bf16),
            pltpu.VMEM((U, TILE, F), bf16),
            pltpu.VMEM((B, TILE, F), bf16),
            pltpu.VMEM((B, TILE, F), bf16),
            pltpu.VMEM((B, TILE, F), f32),
            pltpu.VMEM((B, TILE, F), f32),
            pltpu.VMEM((B, TILE, F), bf16),
            pltpu.VMEM((B, TILE, F), f32),
            pltpu.VMEM((B, TILE, F), bf16),
            pltpu.VMEM((U, TILE, F), f32),
            pltpu.VMEM((F, F), f32),
            pltpu.VMEM((G, R, F), bf16),
            pltpu.VMEM((G, R, F), bf16),
            pltpu.VMEM((R, F), f32),
            pltpu.VMEM((H * N, R, F), f32),
            pltpu.VMEM((F // TILE, U, TILE, TILE), bf16),
            pltpu.VMEM((F // TILE, U, TILE, TILE), bf16),
            dma((W,)), dma((W,)), dma,
            dma((W,)), dma((W,)), dma((F // TILE, W)), dma((F // TILE, W)), dma((W,)), dma((W,)),
            dma((G,)), dma((G,)), dma((H * N,)), dma((H * N,)), dma((G,)), dma((G,)),
            dma((F // TILE, 2 * bits)), dma((F // TILE, 2 * bits)), dma((bits,)), dma((bits,)),
            dma((2,)), dma((2,)),
        ],
        compiler_params=pltpu.CompilerParams(
            collective_id=0, has_side_effects=True, vmem_limit_bytes=61 * 1024 * 1024
        ),
        name="hypergraph",
    )(
        table, tile1_source, tile2_source,
        items.reshape(-1, TILE, F), tile1_values, tile2_values, weight,
        bundle_degree.reshape(B, 1, TILE), user_degree.reshape(U, 1, TILE),
        cotangent.reshape(U, TILE, F),
    )
    uout, gw, gb = pl.pallas_call(
        place_kernel,
        out_shape=(
            jax.ShapeDtypeStruct((U, TILE, F), bf16),
            jax.ShapeDtypeStruct((F, F), f32),
            jax.ShapeDtypeStruct((B, TILE, F), bf16),
        ),
        in_specs=[vmem] * 3,
        out_specs=(vmem,) * 3,
        name="place",
    )(users, gw, gb)
    return uout.reshape(U * TILE, F), gw, gb.reshape(B * TILE, F)


def solution(mesh):
    both = ("wide", "narrow")
    in_specs = (
        P(both, None), P(both, None, None), P(both), P(both, None), P(both),
        P(both, None, None), P(both), P(both, None), P(both),
        P(), P(both), P("wide"), P("wide", None),
    )
    out_specs = (P("wide", None), P(), P(both, None))
    return jax.shard_map(local, mesh=mesh, in_specs=in_specs, out_specs=out_specs, check_vma=False)
```

```python
import functools

import jax
import jax.numpy as jnp
from jax import lax
from jax.experimental import pallas as pl
from jax.experimental.pallas import tpu as pltpu
from jax.sharding import PartitionSpec as P

F = 256
TILE = 128
CAP = 2
MESH = pl.DeviceIdType.MESH
f32 = jnp.float32
bf16 = jnp.bfloat16


def plan_kernel(width, tiles1, tiles2, owner1, slot1, owner2, slot2, table, count):
    size = width * CAP

    def clear(i, _):
        table[i] = 0
        table[size + i] = 0
        table[2 * size + i] = -1
        table[3 * size + i] = -1
        return 0

    lax.fori_loop(0, size, clear, 0)

    def reset(i, _):
        count[i] = 0
        return 0

    lax.fori_loop(0, 2 * width, reset, 0)

    def first(t, _):
        owner = owner1[t]
        place = owner * CAP + count[owner]
        count[owner] = count[owner] + 1
        table[place] = t
        table[2 * size + place] = slot1[t]
        return 0

    lax.fori_loop(0, tiles1, first, 0)

    def second(t, _):
        owner = owner2[t]
        place = owner * CAP + count[width + owner]
        count[width + owner] = count[width + owner] + 1
        table[size + place] = t
        table[3 * size + place] = slot2[t]
        table[4 * size + t] = place
        return 0

    lax.fori_loop(0, tiles2, second, 0)


def main_kernel(
    W, N, G, B, U, T2,
    table, source1, source2,
    items, tile1, tile2, weight, bdeg, udeg, cot,
    users, gw_fin, gb_out,
    labs, rlab, slab,
    send_a, send_c, recv_a, recv_b, recv_c,
    inv_u, scaled, relay, half_send, half_recv, acc1, gact, emb, mixed, act, acc2,
    gw_out, gw_send, gw_recv, gw_part, gw_parts,
    red_send, red_recv,
    lab_s, lab_r, copy_sem, a_s, a_r, b_s, b_r, c_s, c_r,
    g1_s, g1_r, g2_s, g2_r, g3_s, g3_r, n_s, n_r, r_s, r_r, h_s, h_r,
):
    w = lax.axis_index("wide")
    n = lax.axis_index("narrow")
    H = W // G
    R = F // G
    SZ = W * CAP
    h, g = w // G, w % G
    Q = W // 2
    side, place_in = w // Q, w % Q
    pair = lax.rem(w + Q, W)
    C = F // TILE
    bits = N.bit_length() - 1

    def up(d):
        return lax.rem(w + d, W)

    def down(d):
        return lax.rem(w - d + W, W)

    def crossing(q):
        other = lax.rem(h * N + n + q, H * N)
        return (other // N) * G + g, other % N

    barrier = pltpu.get_barrier_semaphore()

    def greet(d, _):
        pl.semaphore_signal(barrier, inc=1, device_id=(up(d), n), device_id_type=MESH)
        return 0

    lax.fori_loop(1, W, greet, 0)

    def greet_cross(q, _):
        pl.semaphore_signal(barrier, inc=1, device_id=crossing(q), device_id_type=MESH)
        return 0

    lax.fori_loop(1, H * N, greet_cross, 0)
    if H > 1:
        def greet_group(d, _):
            peer = h * G + lax.rem(g + d, G)
            pl.semaphore_signal(barrier, inc=1, device_id=(peer, n), device_id_type=MESH)
            return 0

        lax.fori_loop(1, G, greet_group, 0)
    lane = lax.broadcasted_iota(jnp.int32, (8, 128), 1)

    def pack(o, _):
        v = jnp.zeros((8, 128), jnp.int32)
        for k in range(CAP):
            v = jnp.where(lane == k, table[2 * SZ + o * CAP + k], v)
            v = jnp.where(lane == CAP + k, table[3 * SZ + o * CAP + k], v)
            far = lax.rem(o + Q, W) * CAP + k
            v = jnp.where(lane == 2 * CAP + k, table[2 * SZ + far], v)
            v = jnp.where(lane == 3 * CAP + k, table[3 * SZ + far], v)
        labs[o] = v
        return 0

    lax.fori_loop(0, W, pack, 0)
    rlab[w] = labs[w]
    pl.semaphore_wait(barrier, W - 1 + H * N - 1 + (G - 1 if H > 1 else 0))

    def remote(src, dst, ss, rs, dev):
        return pltpu.make_async_remote_copy(
            src_ref=src, dst_ref=dst, send_sem=ss, recv_sem=rs, device_id=dev, device_id_type=MESH
        )

    def wide_copy(src, dst, ss, rs, d):
        return remote(src.at[up(d)], dst.at[w], ss.at[d], rs.at[d], (up(d), n))

    def send_labels(d, _):
        wide_copy(labs, rlab, lab_s, lab_r, d).start()
        return 0

    lax.fori_loop(1, W, send_labels, 0)

    spans = []
    size, base = U, 0
    for i in range(bits):
        size //= 2
        bit = (n // (1 << i)) % 2
        peer = n + (1 - 2 * bit) * (1 << i)
        spans.append((base + bit * size, base + (1 - bit) * size, size, peer))
        base = base + bit * size

    def scale(b):
        row = 1.0 / udeg[b].astype(f32)
        inv = jnp.transpose(jnp.broadcast_to(row, (TILE, TILE)))
        inv_u[b] = inv
        for c in range(C):
            cols = slice(c * TILE, (c + 1) * TILE)
            scaled[b, :, cols] = (cot[b, :, cols].astype(f32) * inv).astype(bf16)

    def scale_first(j, _):
        scale(base + j)
        return 0

    def scale_rest(j, _):
        scale(lax.rem(base + j, U))
        return 0

    lax.fori_loop(0, size, scale_first, 0)
    over = remote(
        scaled.at[pl.ds(base, size)], relay.at[pl.ds(base, size)], h_s.at[0], h_r.at[0], (pair, n)
    )
    over.start()

    def mate(d):
        return side * Q + lax.rem(place_in + d, Q)

    def mate_back(d):
        return side * Q + lax.rem(place_in - d + Q, Q)

    def far(o):
        return lax.rem(o + Q, W)

    def near_copy(src, dst, ss, rs, d):
        return remote(src.at[mate(d)], dst.at[w], ss.at[d], rs.at[d], (mate(d), n))

    def far_copy(src, dst, ss, rs, d):
        return remote(src.at[far(mate(d))], dst.at[pair], ss.at[Q + d], rs.at[Q + d], (mate(d), n))

    def term1(o, k):
        t = table[o * CAP + k]
        return jnp.dot(tile1[t], items[source1[t]], preferred_element_type=f32).astype(bf16)

    def put(buffer, o, k, value):
        for c in range(C):
            buffer[o, c, k] = value[:, c * TILE:(c + 1) * TILE]

    def send_far1(d, _):
        o = far(mate(d))
        for k in range(CAP):
            put(send_a, o, k, term1(o, k))
        far_copy(send_a, recv_a, a_s, a_r, d).start()
        return 0

    def make_near1(d, _):
        o = mate(d)
        for k in range(CAP):
            put(send_a, o, k, term1(o, k))
        return 0

    lax.fori_loop(1, Q, send_far1, 0)
    lax.fori_loop(1, Q, make_near1, 0)
    for k in range(CAP):
        put(recv_a, pair, k, term1(pair, k))
        put(recv_a, w, k, term1(w, k))
    lax.fori_loop(size, U, scale_rest, 0)

    def release_near1(d, _):
        far_copy(send_a, recv_a, a_s, a_r, d).wait_send()
        near_copy(send_a, recv_a, a_s, a_r, d).start()
        return 0

    lax.fori_loop(1, Q, release_near1, 0)

    def wait_labels(d, _):
        c = wide_copy(labs, rlab, lab_s, lab_r, d)
        c.wait_send()
        c.wait_recv()
        return 0

    lax.fori_loop(1, W, wait_labels, 0)
    local = pltpu.make_async_copy(rlab.at[:, pl.ds(0, 1), :], slab, copy_sem)
    local.start()
    local.wait()

    ROWS = 32

    def add_blocks(acc, recv, place, o, start, blocks, columns=range(C)):
        labels = [slab[o, 0, start + k] for k in range(CAP)]

        def part(r, _):
            rows = pl.ds(pl.multiple_of(r * ROWS, ROWS), ROWS)
            for c in columns:
                cols = slice(c * TILE, (c + 1) * TILE)
                xs = [recv[place, c, k, rows, :].astype(f32) for k in range(CAP)]
                for b in range(blocks):
                    total = acc[b, rows, cols]
                    for k in range(CAP):
                        total = total + xs[k] * (labels[k] == b).astype(f32)
                    acc[b, rows, cols] = total
            return 0

        lax.fori_loop(0, TILE // ROWS, part, 0)

    gact[...] = jnp.zeros_like(gact)
    add_blocks(gact, recv_a, pair, w, 2 * CAP, B)

    def collect_far(d, _):
        far_copy(send_a, recv_a, a_s, a_r, d).wait_recv()
        o = mate_back(d)
        add_blocks(gact, recv_a, far(o), o, 2 * CAP, B)
        return 0

    lax.fori_loop(1, Q, collect_far, 0)
    half_send[...] = gact[...].astype(bf16)
    across = remote(half_send, half_recv, h_s.at[1], h_r.at[1], (pair, n))
    across.start()

    def near_block(o, k):
        return scaled[jnp.maximum(slab[o, 0, CAP + k], 0)]

    def far_block(o, k):
        return relay[jnp.maximum(slab[o, 0, 3 * CAP + k], 0)]

    def send_near_replies(d, _):
        o = mate(d)
        for k in range(CAP):
            send_c[o, k] = near_block(o, k)
        near_copy(send_c, recv_c, c_s, c_r, d).start()
        return 0

    def send_far_replies(d, _):
        o = mate(d)
        for k in range(CAP):
            send_c[far(o), k] = far_block(o, k)
        far_copy(send_c, recv_c, c_s, c_r, d).start()
        return 0

    def relay_copy(i):
        mine, _, many, peer = spans[i]
        span = relay.at[pl.ds(mine, many)]
        return remote(span, span, r_s.at[i], r_r.at[i], (w, peer))

    over.wait_recv()
    relay_copy(bits - 1).start()
    lax.fori_loop(1, Q, send_near_replies, 0)
    for k in range(CAP):
        recv_c[w, k] = near_block(w, k)

    acc1[...] = jnp.zeros_like(acc1)
    add_blocks(acc1, recv_a, w, w, 0, B)

    def collect_near(d, _):
        near_copy(send_a, recv_a, a_s, a_r, d).wait_recv()
        o = mate_back(d)
        add_blocks(acc1, recv_a, o, o, 0, B)
        return 0

    lax.fori_loop(1, Q, collect_near, 0)
    for i in range(bits - 1, 0, -1):
        relay_copy(i).wait_recv()
        relay_copy(i).wait_send()
        relay_copy(i - 1).start()
    across.wait_recv()
    acc1[...] += half_recv[...].astype(f32)

    def transform(b, _):
        row = 1.0 / bdeg[b].astype(f32)
        inv = jnp.transpose(jnp.broadcast_to(row, (TILE, TILE)))
        for c in range(F // TILE):
            cols = slice(c * TILE, (c + 1) * TILE)
            emb[b, :, cols] = (acc1[b, :, cols] * inv).astype(bf16)
        m = jnp.dot(emb[b], weight[...], preferred_element_type=f32)
        mixed[b] = m
        act[b] = (m / (1.0 + jnp.exp(-m))).astype(bf16)
        return 0

    lax.fori_loop(0, B, transform, 0)

    def term2(o, k):
        t = table[SZ + o * CAP + k]
        return jnp.dot(tile2[t], act[source2[t]], preferred_element_type=f32).astype(bf16)

    def free_a(d, _):
        near_copy(send_a, recv_a, a_s, a_r, d).wait_send()
        return 0

    lax.fori_loop(1, Q, free_a, 0)

    def column(c):
        return slice(c * TILE, (c + 1) * TILE)

    def user_copy(c, d):
        return remote(
            send_a.at[up(d), c], recv_b.at[w, c],
            b_s.at[c, d], b_r.at[c, d], (up(d), n),
        )

    def send_terms2(d, _):
        o = up(d)
        for k in range(CAP):
            put(send_a, o, k, term2(o, k))
        user_copy(0, d).start()
        return 0

    lax.fori_loop(1, W, send_terms2, 0)
    for k in range(CAP):
        put(recv_b, w, k, term2(w, k))

    relay_copy(0).wait_recv()
    relay_copy(0).wait_send()
    lax.fori_loop(1, Q, send_far_replies, 0)
    for k in range(CAP):
        recv_c[pair, k] = far_block(w, k)

    def send_later(d, _):
        user_copy(0, d).wait_send()
        for c in range(1, C):
            user_copy(c, d).start()
        return 0

    lax.fori_loop(1, W, send_later, 0)

    def wait_replies(d, _):
        for c in (near_copy(send_c, recv_c, c_s, c_r, d), far_copy(send_c, recv_c, c_s, c_r, d)):
            c.wait_recv()
            c.wait_send()
        return 0

    acc2[...] = jnp.zeros_like(acc2)
    add_blocks(acc2, recv_b, w, w, CAP, U)

    def group(d):
        return lax.rem(g + d, G)

    def group_copy1(d):
        return remote(
            gw_send.at[group(d)], gw_recv.at[g], g1_s.at[d], g1_r.at[d], (h * G + group(d), n)
        )

    def cross_copy(q):
        return remote(gw_part, gw_parts.at[h * N + n], g2_s.at[q], g2_r.at[q], crossing(q))

    def group_copy3(d):
        return remote(
            gw_fin.at[g], gw_fin.at[g], g3_s.at[d], g3_r.at[d], (h * G + group(d), n)
        )

    def start_all(copy, size):
        def go(d, _):
            copy(d).start()
            return 0

        lax.fori_loop(1, size, go, 0)

    def wait_all(copy, size):
        def go(d, _):
            c = copy(d)
            c.wait_recv()
            c.wait_send()
            return 0

        lax.fori_loop(1, size, go, 0)

    def collect2(c):
        def go(d, _):
            user_copy(c, d).wait_recv()
            add_blocks(acc2, recv_b, down(d), down(d), CAP, U, [c])
            return 0

        return go

    def halve_copy(c, i):
        _, theirs, many, peer = spans[i]
        return remote(
            red_send.at[c, pl.ds(theirs, many)], red_recv.at[c, pl.ds(U - 2 * many, many)],
            n_s.at[c, i], n_r.at[c, i], (w, peer),
        )

    def double_copy(c, i):
        mine, _, many, peer = spans[i]
        span = users.at[c, pl.ds(mine, many)]
        return remote(span, span, n_s.at[c, bits + i], n_r.at[c, bits + i], (w, peer))

    def halve_start(c, i):
        _, theirs, many, _ = spans[i]

        def ready(j, _):
            red_send[c, theirs + j] = acc2[theirs + j, :, column(c)].astype(bf16)
            return 0

        lax.fori_loop(0, many, ready, 0)
        halve_copy(c, i).start()

    def halve_end(c, i):
        mine, _, many, _ = spans[i]
        x = halve_copy(c, i)
        x.wait_recv()
        x.wait_send()

        def add(j, _):
            acc2[mine + j, :, column(c)] += red_recv[c, U - 2 * many + j].astype(f32)
            return 0

        lax.fori_loop(0, many, add, 0)

    def divide(c):
        def go(j, _):
            b = base + j
            users[c, b] = (acc2[b, :, column(c)] * inv_u[b]).astype(bf16)
            return 0

        lax.fori_loop(0, size, go, 0)

    def double_end(c, i):
        x = double_copy(c, i)
        x.wait_recv()
        x.wait_send()

    def narrow_step(c, step):
        if step < bits:
            if step > 0:
                halve_end(c, step - 1)
            halve_start(c, step)
        elif step < 2 * bits:
            i = 2 * bits - 1 - step
            if step == bits:
                halve_end(c, bits - 1)
                divide(c)
            else:
                double_end(c, i + 1)
            double_copy(c, i).start()
        else:
            double_end(c, 0)

    lax.fori_loop(1, W, collect2(0), 0)
    narrow_step(0, 0)

    gact[...] = jnp.zeros_like(gact)
    lax.fori_loop(1, Q, wait_replies, 0)

    def back(t, _):
        place = table[4 * SZ + t]
        block = recv_c[place // CAP, place % CAP]
        x = lax.dot_general(
            tile2[t], block, (((0,), (0,)), ((), ())), preferred_element_type=f32
        )
        x = x.astype(bf16).astype(f32)
        for b in range(B):
            gact[b] += x * (source2[t] == b).astype(f32)
        return 0

    lax.fori_loop(0, T2, back, 0)
    narrow_step(0, 1)
    def finish(b, total):
        m = mixed[b]
        s = 1.0 / (1.0 + jnp.exp(-m))
        gm = (gact[b] * s * (1.0 + m * (1.0 - s))).astype(bf16)
        gb_out[b] = lax.dot_general(
            gm, weight[...], (((1,), (1,)), ((), ())), preferred_element_type=f32
        ).astype(bf16)
        gw_out[...] += lax.dot_general(
            emb[b], gm, (((0,), (0,)), ((), ())), preferred_element_type=f32
        )
        return total

    gw_out[...] = jnp.zeros_like(gw_out)
    lax.fori_loop(0, B, finish, 0)

    for i in range(G):
        gw_send[i] = gw_out[i * R:(i + 1) * R, :].astype(bf16)

    start_all(group_copy1, G)
    gw_recv[g] = gw_send[g]
    steps = 2 * bits
    narrow_step(0, 2)
    wait_all(group_copy1, G)
    part = gw_recv[0].astype(f32)
    for i in range(1, G):
        part = part + gw_recv[i].astype(f32)
    gw_part[...] = part
    gw_parts[h * N + n] = part
    start_all(cross_copy, H * N)
    for c in range(1, C):
        for step in range(1, steps + 1):
            if step > 2 or c > 1:
                narrow_step(c - 1, step)
            if step == 3 and c == 1:
                wait_all(cross_copy, H * N)
                part = gw_parts[0]
                for i in range(1, H * N):
                    part = part + gw_parts[i]
                gw_fin[g] = part.astype(bf16)
                start_all(group_copy3, G)
            lo = 1 + (W - 1) * (step - 1) // steps
            hi = 1 + (W - 1) * step // steps
            lax.fori_loop(lo, hi, collect2(c), 0)
        narrow_step(c, 0)
    for step in range(1, steps + 1):
        narrow_step(C - 1, step)

    def free_b(d, _):
        for c in range(1, C):
            user_copy(c, d).wait_send()
        return 0

    over.wait_send()
    across.wait_send()
    lax.fori_loop(1, W, free_b, 0)
    wait_all(group_copy3, G)


def place_kernel(users, gw, gb, x, y, z):
    columns, blocks = users.shape[0], users.shape[1]
    rows = gw.shape[1]

    def block(b, _):
        for c in range(columns):
            x[b, :, c * TILE:(c + 1) * TILE] = users[c, b]
        return 0

    lax.fori_loop(0, blocks, block, 0)
    for i in range(gw.shape[0]):
        y[i * rows:(i + 1) * rows, :] = gw[i].astype(f32)
    z[...] = gb[...]


def local(
    items, tile1_values, tile1_source, tile1_owner, tile1_slot,
    tile2_values, tile2_source, tile2_owner, tile2_slot,
    weight, bundle_degree, user_degree, cotangent,
):
    W, N = lax.axis_size("wide"), lax.axis_size("narrow")
    G = min(W, 8)
    H = W // G
    B, U = bundle_degree.shape[0] // TILE, user_degree.shape[0] // TILE
    T1, T2 = tile1_values.shape[0], tile2_values.shape[0]
    R = F // G
    smem = pl.BlockSpec(memory_space=pltpu.SMEM)
    vmem = pl.BlockSpec(memory_space=pltpu.VMEM)
    table = pl.pallas_call(
        functools.partial(plan_kernel, W, T1, T2),
        out_shape=jax.ShapeDtypeStruct((4 * W * CAP + T2,), jnp.int32),
        in_specs=[smem] * 4,
        out_specs=smem,
        scratch_shapes=[pltpu.SMEM((2 * W,), jnp.int32)],
        name="plan",
    )(tile1_owner.reshape(-1), tile1_slot, tile2_owner.reshape(-1), tile2_slot)
    dma = pltpu.SemaphoreType.DMA
    bits = N.bit_length() - 1
    slots = (W, CAP, TILE, F)
    halves = (W, F // TILE, CAP, TILE, TILE)
    users, gw, gb = pl.pallas_call(
        functools.partial(main_kernel, W, N, G, B, U, T2),
        out_shape=(
            jax.ShapeDtypeStruct((F // TILE, U, TILE, TILE), bf16),
            jax.ShapeDtypeStruct((G, R, F), bf16),
            jax.ShapeDtypeStruct((B, TILE, F), bf16),
        ),
        in_specs=[smem] * 3 + [vmem] * 7,
        out_specs=(vmem,) * 3,
        scratch_shapes=[
            pltpu.VMEM((W, 8, 128), jnp.int32),
            pltpu.VMEM((W, 8, 128), jnp.int32),
            pltpu.SMEM((W, 1, 128), jnp.int32),
            pltpu.VMEM(halves, bf16),
            pltpu.VMEM(slots, bf16),
            pltpu.VMEM(halves, bf16),
            pltpu.VMEM(halves, bf16),
            pltpu.VMEM(slots, bf16),
            pltpu.VMEM((U, TILE, TILE), f32),
            pltpu.VMEM((U, TILE, F), bf16),
            pltpu.VMEM((U, TILE, F), bf16),
            pltpu.VMEM((B, TILE, F), bf16),
            pltpu.VMEM((B, TILE, F), bf16),
            pltpu.VMEM((B, TILE, F), f32),
            pltpu.VMEM((B, TILE, F), f32),
            pltpu.VMEM((B, TILE, F), bf16),
            pltpu.VMEM((B, TILE, F), f32),
            pltpu.VMEM((B, TILE, F), bf16),
            pltpu.VMEM((U, TILE, F), f32),
            pltpu.VMEM((F, F), f32),
            pltpu.VMEM((G, R, F), bf16),
            pltpu.VMEM((G, R, F), bf16),
            pltpu.VMEM((R, F), f32),
            pltpu.VMEM((H * N, R, F), f32),
            pltpu.VMEM((F // TILE, U, TILE, TILE), bf16),
            pltpu.VMEM((F // TILE, U, TILE, TILE), bf16),
            dma((W,)), dma((W,)), dma,
            dma((W,)), dma((W,)), dma((F // TILE, W)), dma((F // TILE, W)), dma((W,)), dma((W,)),
            dma((G,)), dma((G,)), dma((H * N,)), dma((H * N,)), dma((G,)), dma((G,)),
            dma((F // TILE, 2 * bits)), dma((F // TILE, 2 * bits)), dma((bits,)), dma((bits,)),
            dma((2,)), dma((2,)),
        ],
        compiler_params=pltpu.CompilerParams(
            collective_id=0, has_side_effects=True, vmem_limit_bytes=61 * 1024 * 1024
        ),
        name="hypergraph",
    )(
        table, tile1_source, tile2_source,
        items.reshape(-1, TILE, F), tile1_values, tile2_values, weight,
        bundle_degree.reshape(B, 1, TILE), user_degree.reshape(U, 1, TILE),
        cotangent.reshape(U, TILE, F),
    )
    uout, gw, gb = pl.pallas_call(
        place_kernel,
        out_shape=(
            jax.ShapeDtypeStruct((U, TILE, F), bf16),
            jax.ShapeDtypeStruct((F, F), f32),
            jax.ShapeDtypeStruct((B, TILE, F), bf16),
        ),
        in_specs=[vmem] * 3,
        out_specs=(vmem,) * 3,
        name="place",
    )(users, gw, gb)
    return uout.reshape(U * TILE, F), gw, gb.reshape(B * TILE, F)


def solution(mesh):
    both = ("wide", "narrow")
    in_specs = (
        P(both, None), P(both, None, None), P(both), P(both, None), P(both),
        P(both, None, None), P(both), P(both, None), P(both),
        P(), P(both), P("wide"), P("wide", None),
    )
    out_specs = (P("wide", None), P(), P(both, None))
    return jax.shard_map(local, mesh=mesh, in_specs=in_specs, out_specs=out_specs, check_vma=False)
```

```python
import functools

import jax
import jax.numpy as jnp
from jax import lax
from jax.experimental import pallas as pl
from jax.experimental.pallas import tpu as pltpu
from jax.sharding import PartitionSpec as P

F = 256
TILE = 128
CAP = 2
MESH = pl.DeviceIdType.MESH
f32 = jnp.float32
bf16 = jnp.bfloat16


def plan_kernel(width, tiles1, tiles2, owner1, slot1, owner2, slot2, table, count):
    size = width * CAP

    def clear(i, _):
        table[i] = 0
        table[size + i] = 0
        table[2 * size + i] = -1
        table[3 * size + i] = -1
        return 0

    lax.fori_loop(0, size, clear, 0)

    def reset(i, _):
        count[i] = 0
        return 0

    lax.fori_loop(0, 2 * width, reset, 0)

    def first(t, _):
        owner = owner1[t]
        place = owner * CAP + count[owner]
        count[owner] = count[owner] + 1
        table[place] = t
        table[2 * size + place] = slot1[t]
        return 0

    lax.fori_loop(0, tiles1, first, 0)

    def second(t, _):
        owner = owner2[t]
        place = owner * CAP + count[width + owner]
        count[width + owner] = count[width + owner] + 1
        table[size + place] = t
        table[3 * size + place] = slot2[t]
        table[4 * size + t] = place
        return 0

    lax.fori_loop(0, tiles2, second, 0)


def main_kernel(
    W, N, G, B, U, T2,
    table, source1, source2,
    items, tile1, tile2, weight, bdeg, udeg, cot,
    users, gw_fin, gb_out,
    labs, rlab, slab,
    send_a, send_c, recv_a, recv_b, recv_c,
    inv_u, scaled, relay, half_send, half_recv, acc1, gact, emb, mixed, act, acc2,
    gw_out, gw_send, gw_recv, gw_part, gw_parts,
    red_send, red_recv,
    lab_s, lab_r, copy_sem, a_s, a_r, b_s, b_r, c_s, c_r,
    g1_s, g1_r, g2_s, g2_r, g3_s, g3_r, n_s, n_r, r_s, r_r, h_s, h_r,
):
    w = lax.axis_index("wide")
    n = lax.axis_index("narrow")
    H = W // G
    R = F // G
    SZ = W * CAP
    h, g = w // G, w % G
    Q = W // 2
    side, place_in = w // Q, w % Q
    pair = lax.rem(w + Q, W)
    C = F // TILE
    bits = N.bit_length() - 1

    def up(d):
        return lax.rem(w + d, W)

    def down(d):
        return lax.rem(w - d + W, W)

    def crossing(q):
        other = lax.rem(h * N + n + q, H * N)
        return (other // N) * G + g, other % N

    barrier = pltpu.get_barrier_semaphore()

    def greet(d, _):
        pl.semaphore_signal(barrier, inc=1, device_id=(up(d), n), device_id_type=MESH)
        return 0

    lax.fori_loop(1, W, greet, 0)

    def greet_cross(q, _):
        pl.semaphore_signal(barrier, inc=1, device_id=crossing(q), device_id_type=MESH)
        return 0

    lax.fori_loop(1, H * N, greet_cross, 0)
    if H > 1:
        def greet_group(d, _):
            peer = h * G + lax.rem(g + d, G)
            pl.semaphore_signal(barrier, inc=1, device_id=(peer, n), device_id_type=MESH)
            return 0

        lax.fori_loop(1, G, greet_group, 0)
    lane = lax.broadcasted_iota(jnp.int32, (8, 128), 1)

    def pack(o, _):
        v = jnp.zeros((8, 128), jnp.int32)
        for k in range(CAP):
            v = jnp.where(lane == k, table[2 * SZ + o * CAP + k], v)
            v = jnp.where(lane == CAP + k, table[3 * SZ + o * CAP + k], v)
            far = lax.rem(o + Q, W) * CAP + k
            v = jnp.where(lane == 2 * CAP + k, table[2 * SZ + far], v)
            v = jnp.where(lane == 3 * CAP + k, table[3 * SZ + far], v)
        labs[o] = v
        return 0

    lax.fori_loop(0, W, pack, 0)
    rlab[w] = labs[w]
    pl.semaphore_wait(barrier, W - 1 + H * N - 1 + (G - 1 if H > 1 else 0))

    def remote(src, dst, ss, rs, dev):
        return pltpu.make_async_remote_copy(
            src_ref=src, dst_ref=dst, send_sem=ss, recv_sem=rs, device_id=dev, device_id_type=MESH
        )

    def wide_copy(src, dst, ss, rs, d):
        return remote(src.at[up(d)], dst.at[w], ss.at[d], rs.at[d], (up(d), n))

    def send_labels(d, _):
        wide_copy(labs, rlab, lab_s, lab_r, d).start()
        return 0

    lax.fori_loop(1, W, send_labels, 0)

    spans = []
    size, base = U, 0
    for i in range(bits):
        size //= 2
        bit = (n // (1 << i)) % 2
        peer = n + (1 - 2 * bit) * (1 << i)
        spans.append((base + bit * size, base + (1 - bit) * size, size, peer))
        base = base + bit * size

    def scale(b):
        row = 1.0 / udeg[b].astype(f32)
        inv = jnp.transpose(jnp.broadcast_to(row, (TILE, TILE)))
        inv_u[b] = inv
        for c in range(C):
            cols = slice(c * TILE, (c + 1) * TILE)
            scaled[b, :, cols] = (cot[b, :, cols].astype(f32) * inv).astype(bf16)

    def scale_first(j, _):
        scale(base + j)
        return 0

    def scale_rest(j, _):
        scale(lax.rem(base + j, U))
        return 0


    def mate(d):
        return side * Q + lax.rem(place_in + d, Q)

    def mate_back(d):
        return side * Q + lax.rem(place_in - d + Q, Q)

    def far(o):
        return lax.rem(o + Q, W)

    def near_copy(src, dst, ss, rs, d):
        return remote(src.at[mate(d)], dst.at[w], ss.at[d], rs.at[d], (mate(d), n))

    def far_copy(src, dst, ss, rs, d):
        return remote(src.at[far(mate(d))], dst.at[pair], ss.at[Q + d], rs.at[Q + d], (mate(d), n))

    def term1(o, k):
        t = table[o * CAP + k]
        return jnp.dot(tile1[t], items[source1[t]], preferred_element_type=f32).astype(bf16)

    def put(buffer, o, k, value):
        for c in range(C):
            buffer[o, c, k] = value[:, c * TILE:(c + 1) * TILE]

    def send_far1(d, _):
        o = far(mate(d))
        for k in range(CAP):
            put(send_a, o, k, term1(o, k))
        far_copy(send_a, recv_a, a_s, a_r, d).start()
        return 0

    def make_near1(d, _):
        o = mate(d)
        for k in range(CAP):
            put(send_a, o, k, term1(o, k))
        return 0

    lax.fori_loop(1, Q, send_far1, 0)
    lax.fori_loop(0, size, scale_first, 0)
    over = remote(
        scaled.at[pl.ds(base, size)], relay.at[pl.ds(base, size)], h_s.at[0], h_r.at[0], (pair, n)
    )
    over.start()
    lax.fori_loop(1, Q, make_near1, 0)
    for k in range(CAP):
        put(recv_a, pair, k, term1(pair, k))
        put(recv_a, w, k, term1(w, k))
    lax.fori_loop(size, U, scale_rest, 0)

    def release_near1(d, _):
        far_copy(send_a, recv_a, a_s, a_r, d).wait_send()
        near_copy(send_a, recv_a, a_s, a_r, d).start()
        return 0

    lax.fori_loop(1, Q, release_near1, 0)

    def wait_labels(d, _):
        c = wide_copy(labs, rlab, lab_s, lab_r, d)
        c.wait_send()
        c.wait_recv()
        return 0

    lax.fori_loop(1, W, wait_labels, 0)
    local = pltpu.make_async_copy(rlab.at[:, pl.ds(0, 1), :], slab, copy_sem)
    local.start()
    local.wait()

    ROWS = 32

    def add_blocks(acc, recv, place, o, start, blocks, columns=range(C)):
        labels = [slab[o, 0, start + k] for k in range(CAP)]

        def part(r, _):
            rows = pl.ds(pl.multiple_of(r * ROWS, ROWS), ROWS)
            for c in columns:
                cols = slice(c * TILE, (c + 1) * TILE)
                xs = [recv[place, c, k, rows, :].astype(f32) for k in range(CAP)]
                for b in range(blocks):
                    total = acc[b, rows, cols]
                    for k in range(CAP):
                        total = total + xs[k] * (labels[k] == b).astype(f32)
                    acc[b, rows, cols] = total
            return 0

        lax.fori_loop(0, TILE // ROWS, part, 0)

    gact[...] = jnp.zeros_like(gact)
    add_blocks(gact, recv_a, pair, w, 2 * CAP, B)

    def collect_far(d, _):
        far_copy(send_a, recv_a, a_s, a_r, d).wait_recv()
        o = mate_back(d)
        add_blocks(gact, recv_a, far(o), o, 2 * CAP, B)
        return 0

    lax.fori_loop(1, Q, collect_far, 0)
    half_send[...] = gact[...].astype(bf16)
    across = remote(half_send, half_recv, h_s.at[1], h_r.at[1], (pair, n))
    across.start()

    def near_block(o, k):
        return scaled[jnp.maximum(slab[o, 0, CAP + k], 0)]

    def far_block(o, k):
        return relay[jnp.maximum(slab[o, 0, 3 * CAP + k], 0)]

    def send_near_replies(d, _):
        o = mate(d)
        for k in range(CAP):
            send_c[o, k] = near_block(o, k)
        near_copy(send_c, recv_c, c_s, c_r, d).start()
        return 0

    def send_far_replies(d, _):
        o = mate(d)
        for k in range(CAP):
            send_c[far(o), k] = far_block(o, k)
        far_copy(send_c, recv_c, c_s, c_r, d).start()
        return 0

    def relay_copy(i):
        mine, _, many, peer = spans[i]
        span = relay.at[pl.ds(mine, many)]
        return remote(span, span, r_s.at[i], r_r.at[i], (w, peer))

    over.wait_recv()
    relay_copy(bits - 1).start()
    lax.fori_loop(1, Q, send_near_replies, 0)
    for k in range(CAP):
        recv_c[w, k] = near_block(w, k)

    acc1[...] = jnp.zeros_like(acc1)
    add_blocks(acc1, recv_a, w, w, 0, B)

    def collect_near(d, _):
        near_copy(send_a, recv_a, a_s, a_r, d).wait_recv()
        o = mate_back(d)
        add_blocks(acc1, recv_a, o, o, 0, B)
        return 0

    lax.fori_loop(1, Q, collect_near, 0)
    for i in range(bits - 1, 0, -1):
        relay_copy(i).wait_recv()
        relay_copy(i).wait_send()
        relay_copy(i - 1).start()
    across.wait_recv()
    acc1[...] += half_recv[...].astype(f32)

    def transform(b, _):
        row = 1.0 / bdeg[b].astype(f32)
        inv = jnp.transpose(jnp.broadcast_to(row, (TILE, TILE)))
        for c in range(F // TILE):
            cols = slice(c * TILE, (c + 1) * TILE)
            emb[b, :, cols] = (acc1[b, :, cols] * inv).astype(bf16)
        m = jnp.dot(emb[b], weight[...], preferred_element_type=f32)
        mixed[b] = m
        act[b] = (m / (1.0 + jnp.exp(-m))).astype(bf16)
        return 0

    lax.fori_loop(0, B, transform, 0)

    def term2(o, k):
        t = table[SZ + o * CAP + k]
        return jnp.dot(tile2[t], act[source2[t]], preferred_element_type=f32).astype(bf16)

    def free_a(d, _):
        near_copy(send_a, recv_a, a_s, a_r, d).wait_send()
        return 0

    lax.fori_loop(1, Q, free_a, 0)

    def column(c):
        return slice(c * TILE, (c + 1) * TILE)

    def user_copy(c, d):
        return remote(
            send_a.at[up(d), c], recv_b.at[w, c],
            b_s.at[c, d], b_r.at[c, d], (up(d), n),
        )

    def send_terms2(d, _):
        o = up(d)
        for k in range(CAP):
            put(send_a, o, k, term2(o, k))
        user_copy(0, d).start()
        return 0

    lax.fori_loop(1, W, send_terms2, 0)
    for k in range(CAP):
        put(recv_b, w, k, term2(w, k))

    relay_copy(0).wait_recv()
    relay_copy(0).wait_send()
    lax.fori_loop(1, Q, send_far_replies, 0)
    for k in range(CAP):
        recv_c[pair, k] = far_block(w, k)

    def send_later(d, _):
        user_copy(0, d).wait_send()
        for c in range(1, C):
            user_copy(c, d).start()
        return 0

    lax.fori_loop(1, W, send_later, 0)

    def wait_replies(d, _):
        for c in (near_copy(send_c, recv_c, c_s, c_r, d), far_copy(send_c, recv_c, c_s, c_r, d)):
            c.wait_recv()
            c.wait_send()
        return 0

    acc2[...] = jnp.zeros_like(acc2)
    add_blocks(acc2, recv_b, w, w, CAP, U)

    def group(d):
        return lax.rem(g + d, G)

    def group_copy1(d):
        return remote(
            gw_send.at[group(d)], gw_recv.at[g], g1_s.at[d], g1_r.at[d], (h * G + group(d), n)
        )

    def cross_copy(q):
        return remote(gw_part, gw_parts.at[h * N + n], g2_s.at[q], g2_r.at[q], crossing(q))

    def group_copy3(d):
        return remote(
            gw_fin.at[g], gw_fin.at[g], g3_s.at[d], g3_r.at[d], (h * G + group(d), n)
        )

    def start_all(copy, size):
        def go(d, _):
            copy(d).start()
            return 0

        lax.fori_loop(1, size, go, 0)

    def wait_all(copy, size):
        def go(d, _):
            c = copy(d)
            c.wait_recv()
            c.wait_send()
            return 0

        lax.fori_loop(1, size, go, 0)

    def collect2(c):
        def go(d, _):
            user_copy(c, d).wait_recv()
            add_blocks(acc2, recv_b, down(d), down(d), CAP, U, [c])
            return 0

        return go

    def halve_copy(c, i):
        _, theirs, many, peer = spans[i]
        return remote(
            red_send.at[c, pl.ds(theirs, many)], red_recv.at[c, pl.ds(U - 2 * many, many)],
            n_s.at[c, i], n_r.at[c, i], (w, peer),
        )

    def double_copy(c, i):
        mine, _, many, peer = spans[i]
        span = users.at[c, pl.ds(mine, many)]
        return remote(span, span, n_s.at[c, bits + i], n_r.at[c, bits + i], (w, peer))

    def halve_start(c, i):
        _, theirs, many, _ = spans[i]

        def ready(j, _):
            red_send[c, theirs + j] = acc2[theirs + j, :, column(c)].astype(bf16)
            return 0

        lax.fori_loop(0, many, ready, 0)
        halve_copy(c, i).start()

    def halve_end(c, i):
        mine, _, many, _ = spans[i]
        x = halve_copy(c, i)
        x.wait_recv()
        x.wait_send()

        def add(j, _):
            acc2[mine + j, :, column(c)] += red_recv[c, U - 2 * many + j].astype(f32)
            return 0

        lax.fori_loop(0, many, add, 0)

    def divide(c):
        def go(j, _):
            b = base + j
            users[c, b] = (acc2[b, :, column(c)] * inv_u[b]).astype(bf16)
            return 0

        lax.fori_loop(0, size, go, 0)

    def double_end(c, i):
        x = double_copy(c, i)
        x.wait_recv()
        x.wait_send()

    def narrow_step(c, step):
        if step < bits:
            if step > 0:
                halve_end(c, step - 1)
            halve_start(c, step)
        elif step < 2 * bits:
            i = 2 * bits - 1 - step
            if step == bits:
                halve_end(c, bits - 1)
                divide(c)
            else:
                double_end(c, i + 1)
            double_copy(c, i).start()
        else:
            double_end(c, 0)

    lax.fori_loop(1, W, collect2(0), 0)
    narrow_step(0, 0)

    gact[...] = jnp.zeros_like(gact)
    lax.fori_loop(1, Q, wait_replies, 0)

    def back(t, _):
        place = table[4 * SZ + t]
        block = recv_c[place // CAP, place % CAP]
        x = lax.dot_general(
            tile2[t], block, (((0,), (0,)), ((), ())), preferred_element_type=f32
        )
        x = x.astype(bf16).astype(f32)
        for b in range(B):
            gact[b] += x * (source2[t] == b).astype(f32)
        return 0

    lax.fori_loop(0, T2, back, 0)
    narrow_step(0, 1)
    def finish(b, total):
        m = mixed[b]
        s = 1.0 / (1.0 + jnp.exp(-m))
        gm = (gact[b] * s * (1.0 + m * (1.0 - s))).astype(bf16)
        gb_out[b] = lax.dot_general(
            gm, weight[...], (((1,), (1,)), ((), ())), preferred_element_type=f32
        ).astype(bf16)
        gw_out[...] += lax.dot_general(
            emb[b], gm, (((0,), (0,)), ((), ())), preferred_element_type=f32
        )
        return total

    gw_out[...] = jnp.zeros_like(gw_out)
    lax.fori_loop(0, B, finish, 0)

    for i in range(G):
        gw_send[i] = gw_out[i * R:(i + 1) * R, :].astype(bf16)

    start_all(group_copy1, G)
    gw_recv[g] = gw_send[g]
    steps = 2 * bits
    narrow_step(0, 2)
    wait_all(group_copy1, G)
    part = gw_recv[0].astype(f32)
    for i in range(1, G):
        part = part + gw_recv[i].astype(f32)
    gw_part[...] = part
    gw_parts[h * N + n] = part
    start_all(cross_copy, H * N)
    for c in range(1, C):
        for step in range(1, steps + 1):
            if step > 2 or c > 1:
                narrow_step(c - 1, step)
            if step == 3 and c == 1:
                wait_all(cross_copy, H * N)
                part = gw_parts[0]
                for i in range(1, H * N):
                    part = part + gw_parts[i]
                gw_fin[g] = part.astype(bf16)
                start_all(group_copy3, G)
            lo = 1 + (W - 1) * (step - 1) // steps
            hi = 1 + (W - 1) * step // steps
            lax.fori_loop(lo, hi, collect2(c), 0)
        narrow_step(c, 0)
    for step in range(1, steps + 1):
        narrow_step(C - 1, step)

    def free_b(d, _):
        for c in range(1, C):
            user_copy(c, d).wait_send()
        return 0

    over.wait_send()
    across.wait_send()
    lax.fori_loop(1, W, free_b, 0)
    wait_all(group_copy3, G)


def place_kernel(users, gw, gb, x, y, z):
    columns, blocks = users.shape[0], users.shape[1]
    rows = gw.shape[1]

    def block(b, _):
        for c in range(columns):
            x[b, :, c * TILE:(c + 1) * TILE] = users[c, b]
        return 0

    lax.fori_loop(0, blocks, block, 0)
    for i in range(gw.shape[0]):
        y[i * rows:(i + 1) * rows, :] = gw[i].astype(f32)
    z[...] = gb[...]


def local(
    items, tile1_values, tile1_source, tile1_owner, tile1_slot,
    tile2_values, tile2_source, tile2_owner, tile2_slot,
    weight, bundle_degree, user_degree, cotangent,
):
    W, N = lax.axis_size("wide"), lax.axis_size("narrow")
    G = min(W, 8)
    H = W // G
    B, U = bundle_degree.shape[0] // TILE, user_degree.shape[0] // TILE
    T1, T2 = tile1_values.shape[0], tile2_values.shape[0]
    R = F // G
    smem = pl.BlockSpec(memory_space=pltpu.SMEM)
    vmem = pl.BlockSpec(memory_space=pltpu.VMEM)
    table = pl.pallas_call(
        functools.partial(plan_kernel, W, T1, T2),
        out_shape=jax.ShapeDtypeStruct((4 * W * CAP + T2,), jnp.int32),
        in_specs=[smem] * 4,
        out_specs=smem,
        scratch_shapes=[pltpu.SMEM((2 * W,), jnp.int32)],
        name="plan",
    )(tile1_owner.reshape(-1), tile1_slot, tile2_owner.reshape(-1), tile2_slot)
    dma = pltpu.SemaphoreType.DMA
    bits = N.bit_length() - 1
    slots = (W, CAP, TILE, F)
    halves = (W, F // TILE, CAP, TILE, TILE)
    users, gw, gb = pl.pallas_call(
        functools.partial(main_kernel, W, N, G, B, U, T2),
        out_shape=(
            jax.ShapeDtypeStruct((F // TILE, U, TILE, TILE), bf16),
            jax.ShapeDtypeStruct((G, R, F), bf16),
            jax.ShapeDtypeStruct((B, TILE, F), bf16),
        ),
        in_specs=[smem] * 3 + [vmem] * 7,
        out_specs=(vmem,) * 3,
        scratch_shapes=[
            pltpu.VMEM((W, 8, 128), jnp.int32),
            pltpu.VMEM((W, 8, 128), jnp.int32),
            pltpu.SMEM((W, 1, 128), jnp.int32),
            pltpu.VMEM(halves, bf16),
            pltpu.VMEM(slots, bf16),
            pltpu.VMEM(halves, bf16),
            pltpu.VMEM(halves, bf16),
            pltpu.VMEM(slots, bf16),
            pltpu.VMEM((U, TILE, TILE), f32),
            pltpu.VMEM((U, TILE, F), bf16),
            pltpu.VMEM((U, TILE, F), bf16),
            pltpu.VMEM((B, TILE, F), bf16),
            pltpu.VMEM((B, TILE, F), bf16),
            pltpu.VMEM((B, TILE, F), f32),
            pltpu.VMEM((B, TILE, F), f32),
            pltpu.VMEM((B, TILE, F), bf16),
            pltpu.VMEM((B, TILE, F), f32),
            pltpu.VMEM((B, TILE, F), bf16),
            pltpu.VMEM((U, TILE, F), f32),
            pltpu.VMEM((F, F), f32),
            pltpu.VMEM((G, R, F), bf16),
            pltpu.VMEM((G, R, F), bf16),
            pltpu.VMEM((R, F), f32),
            pltpu.VMEM((H * N, R, F), f32),
            pltpu.VMEM((F // TILE, U, TILE, TILE), bf16),
            pltpu.VMEM((F // TILE, U, TILE, TILE), bf16),
            dma((W,)), dma((W,)), dma,
            dma((W,)), dma((W,)), dma((F // TILE, W)), dma((F // TILE, W)), dma((W,)), dma((W,)),
            dma((G,)), dma((G,)), dma((H * N,)), dma((H * N,)), dma((G,)), dma((G,)),
            dma((F // TILE, 2 * bits)), dma((F // TILE, 2 * bits)), dma((bits,)), dma((bits,)),
            dma((2,)), dma((2,)),
        ],
        compiler_params=pltpu.CompilerParams(
            collective_id=0, has_side_effects=True, vmem_limit_bytes=61 * 1024 * 1024
        ),
        name="hypergraph",
    )(
        table, tile1_source, tile2_source,
        items.reshape(-1, TILE, F), tile1_values, tile2_values, weight,
        bundle_degree.reshape(B, 1, TILE), user_degree.reshape(U, 1, TILE),
        cotangent.reshape(U, TILE, F),
    )
    uout, gw, gb = pl.pallas_call(
        place_kernel,
        out_shape=(
            jax.ShapeDtypeStruct((U, TILE, F), bf16),
            jax.ShapeDtypeStruct((F, F), f32),
            jax.ShapeDtypeStruct((B, TILE, F), bf16),
        ),
        in_specs=[vmem] * 3,
        out_specs=(vmem,) * 3,
        name="place",
    )(users, gw, gb)
    return uout.reshape(U * TILE, F), gw, gb.reshape(B * TILE, F)


def solution(mesh):
    both = ("wide", "narrow")
    in_specs = (
        P(both, None), P(both, None, None), P(both), P(both, None), P(both),
        P(both, None, None), P(both), P(both, None), P(both),
        P(), P(both), P("wide"), P("wide", None),
    )
    out_specs = (P("wide", None), P(), P(both, None))
    return jax.shard_map(local, mesh=mesh, in_specs=in_specs, out_specs=out_specs, check_vma=False)
```
